256 devices in a mesh: row: 8 (over z), col: 32 (over y, x, core).
Axes of the slice: x: 4, y: 4, z: 8, core: 2. Of those that a mesh axis runs over, the one named last changes fastest.
Arguments:
- features: bfloat16 [32, 2048, 256], P('col', 'row'), may hold values from -6 to 6
- weight: bfloat16 [256, 256], replicated, may hold values from -0.375 to 0.375
- cotangent: bfloat16 [65536, 256], P(('row', 'col')), may hold values from -6 to 6
- blk_vals: bfloat16 [8, 32, 192, 128, 128], P('row', 'col'), may hold values from -0.0546875 to 0.0546875
- blk_rows: int32 [8, 32, 192], P('row', 'col'), may hold values from 0 to 63
- blk_cols: int32 [8, 32, 192], P('row', 'col'), may hold values from 0 to 15
- blk_count: int32 [8, 32], P('row', 'col'), may hold values from 24 to 192, as said below
Outputs:
- activated: bfloat16 [65536, 256], P(('row', 'col'))
- grad_weight: float32 [256, 256], replicated
- grad_features: bfloat16 [32, 2048, 256], P('col', 'row')
The draws below stay inside these ranges and needn't reach their ends.
Inputs may be any that keep to these rules, and one draw needn't show every extreme that they name: Only the first blk_count slots of a panel pair are used; a pair whose row and column node ranges intersect uses all 192, every other pair at most 96.
All inputs are finite; a program needn't handle non-finite values.
Results may differ from the reference program's by a relative error of at most 0.0059.
Values may be sent and summed in bfloat16 or wider, within the bound.
No kernel may reach another device: no remote copies, remote signals or barrier semaphores. Data moves between devices by JAX's collectives and lax.ppermute only.
A program may use at most 128 MiB of HBM per device.

```python
import jax
import jax.numpy as jnp
from jax import lax

F = 256
BLOCK = 128
ROWS_DEV = 256
NBLK = 192
NODES = 65536
PANEL_COLS = 2048
BLOCK_ROWS = 64
BLOCK_COLS = 16
N_ROW = 8
N_COL = 32


def layout_draw(key):
    base = jax.random.fold_in(key, 91)
    keys = jax.random.split(base, 6)
    shape = (N_ROW, N_COL, NBLK)
    panel_r = jnp.arange(N_ROW, dtype=jnp.int32)[:, None] + jnp.zeros((N_ROW, N_COL), jnp.int32)
    panel_c = jnp.arange(N_COL, dtype=jnp.int32)[None, :] + jnp.zeros((N_ROW, N_COL), jnp.int32)
    row_low = panel_r * BLOCK_ROWS
    row_high = row_low + BLOCK_ROWS
    col_low = panel_c * BLOCK_COLS
    col_high = col_low + BLOCK_COLS
    lower = jnp.maximum(row_low, col_low)
    upper = jnp.minimum(row_high, col_high)
    near = upper > lower
    span = jnp.maximum(upper - lower, 1)
    diagonal = lower[..., None] + jax.random.randint(keys[0], shape, 0, 1 << 20) % span[..., None]
    near_rows = jnp.clip(diagonal + jax.random.randint(keys[1], shape, -4, 5), row_low[..., None], row_high[..., None] - 1) - row_low[..., None]
    near_cols = jnp.clip(diagonal + jax.random.randint(keys[2], shape, -4, 5), col_low[..., None], col_high[..., None] - 1) - col_low[..., None]
    far_rows = jax.random.randint(keys[3], shape, 0, BLOCK_ROWS)
    far_cols = jax.random.randint(keys[4], shape, 0, BLOCK_COLS)
    rows = jnp.where(near[..., None], near_rows, far_rows).astype(jnp.int32)
    cols = jnp.where(near[..., None], near_cols, far_cols).astype(jnp.int32)
    far_counts = jax.random.randint(keys[5], (N_ROW, N_COL), NBLK // 8, NBLK // 2 + 1)
    counts = jnp.where(near, NBLK, far_counts).astype(jnp.int32)
    return (rows, cols, counts)


def draw_blk_rows(key, part):
    return layout_draw(key)[0]


def draw_blk_cols(key, part):
    return layout_draw(key)[1]


def draw_blk_count(key, part):
    return layout_draw(key)[2]


def steps_of(stream_key, extent, pieces, smallest, high):
    level, own = 1.0, jax.random.fold_in(stream_key, 6)
    for axis_at, shards_of in pieces:
        heights = jnp.exp(jax.random.uniform(jax.random.fold_in(own, axis_at), (shards_of,), jnp.float32, smallest / len(pieces), high / len(pieces)))
        level = level * jnp.repeat(heights, extent[axis_at] // shards_of).reshape([-1 if axis == axis_at else 1 for axis in range(len(extent))])
    return level


def normal_values(stream_key, extent, deviation, limit, shards=(), kind=jnp.bfloat16):
    factor_of = steps_of(stream_key, extent, shards, -0.22, 0.18) if shards else 1.0
    result = jax.random.normal(stream_key, extent, jnp.float32) * deviation * factor_of
    return jnp.minimum(jnp.maximum(result, -limit), limit).astype(kind)


def setup_inputs(seed: int = 0) -> dict:
    splits = jax.random.split(jax.random.key(seed), 8)
    return {
        "features": normal_values(splits[0], (N_COL, PANEL_COLS, F), 1.0, 6.0, ((0, 32), (1, 8))),
        "weight": normal_values(splits[1], (F, F), F ** -0.5, 0.375),
        "cotangent": normal_values(splits[2], (NODES, F), 1.0, 6.0, ((0, 256),)),
        "blk_vals": normal_values(splits[3], (N_ROW, N_COL, NBLK, BLOCK, BLOCK), (NBLK * BLOCK * BLOCK // ROWS_DEV) ** -0.5, 0.0546875, ((0, 8), (1, 32))),
        "blk_rows": draw_blk_rows(jax.random.fold_in(splits[7], 71), 0),
        "blk_cols": draw_blk_cols(jax.random.fold_in(splits[7], 71), 0),
        "blk_count": draw_blk_count(jax.random.fold_in(splits[7], 71), 0),
    }


def reference(features, weight, cotangent, blk_vals, blk_rows, blk_cols, blk_count):
    width = features.shape[-1]
    row_blocks = ROWS_DEV * N_COL // BLOCK
    col_blocks = ROWS_DEV * N_ROW // BLOCK
    slot_ids = jnp.arange(NBLK, dtype=jnp.int32)

    def forward_step(accum, device):
        panel_r = device // N_COL
        panel_c = device % N_COL
        values = blk_vals[panel_r, panel_c].astype(jnp.float32)
        live = (slot_ids < blk_count[panel_r, panel_c]).astype(jnp.float32)
        source = features[panel_c].reshape(col_blocks, BLOCK, width)
        picked = source[blk_cols[panel_r, panel_c]].astype(jnp.float32)
        product = jnp.einsum('bij,bjf->bif', values, picked) * live[:, None, None]
        partial_sum = jax.ops.segment_sum(product, blk_rows[panel_r, panel_c], num_segments=row_blocks)
        return accum.at[panel_r].add(partial_sum), None

    start_fwd = jnp.zeros((N_ROW, row_blocks, BLOCK, width), jnp.float32)
    devices = jnp.arange(N_ROW * N_COL, dtype=jnp.int32)
    total_fwd, unused = lax.scan(forward_step, start_fwd, devices)
    aggregated = total_fwd.reshape(NODES, width).astype(jnp.bfloat16)
    pre = jnp.dot(aggregated, weight, preferred_element_type=jnp.float32)
    sigma = jax.nn.sigmoid(pre)
    activated = (pre * sigma).astype(jnp.bfloat16)
    grad_pre = (cotangent.astype(jnp.float32) * sigma * (1.0 + pre * (1.0 - sigma))).astype(jnp.bfloat16)
    grad_weight = jnp.dot(aggregated.T, grad_pre, preferred_element_type=jnp.float32)
    grad_agg = jnp.dot(grad_pre, weight.T, preferred_element_type=jnp.float32).astype(jnp.bfloat16)
    grad_blocks = grad_agg.reshape(N_ROW, row_blocks, BLOCK, width)

    def backward_step(accum, device):
        panel_r = device // N_COL
        panel_c = device % N_COL
        values = blk_vals[panel_r, panel_c].astype(jnp.float32)
        live = (slot_ids < blk_count[panel_r, panel_c]).astype(jnp.float32)
        picked = grad_blocks[panel_r][blk_rows[panel_r, panel_c]].astype(jnp.float32)
        product = jnp.einsum('bji,bjf->bif', values, picked) * live[:, None, None]
        partial_sum = jax.ops.segment_sum(product, blk_cols[panel_r, panel_c], num_segments=col_blocks)
        return accum.at[panel_c].add(partial_sum), None

    start_bwd = jnp.zeros((N_COL, col_blocks, BLOCK, width), jnp.float32)
    total_bwd, unused_b = lax.scan(backward_step, start_bwd, devices)
    grad_features = total_bwd.reshape(N_COL, ROWS_DEV * N_ROW, width).astype(jnp.bfloat16)
    return (activated, grad_weight, grad_features)
```

```python
import functools

import jax
import jax.numpy as jnp
from jax import lax
from jax.experimental import pallas as pl
from jax.experimental.pallas import tpu as pltpu
from jax.sharding import PartitionSpec as P

BF16 = jnp.bfloat16
F32 = jnp.float32
UNROLL = 4
MIB = 1 << 20


def start_chunks(live, vals_hbm, vals, sems, chunk):
    for piece in range(vals.shape[0] // chunk):

        @pl.when(piece * chunk < live)
        def _():
            part = pl.ds(piece * chunk, chunk)
            pltpu.make_async_copy(vals_hbm.at[part], vals.at[part], sems.at[piece]).start()


def each_live_slot(live, vals_hbm, vals, sems, chunk, one_slot):
    def one_chunk(piece, unused):
        part = pl.ds(piece * chunk, chunk)
        pltpu.make_async_copy(vals_hbm.at[part], vals.at[part], sems.at[piece]).wait()

        def one_group(group, unused):
            for lane in range(UNROLL):
                slot = piece * chunk + group * UNROLL + lane
                one_slot(slot, slot < live)
            return unused

        groups = (jnp.minimum(chunk, live - piece * chunk) + UNROLL - 1) // UNROLL
        return lax.fori_loop(0, groups, one_group, unused)

    lax.fori_loop(0, (live + chunk - 1) // chunk, one_chunk, 0)


def forward_kernel(chunk, place, rows, cols, count, vals_hbm, *refs):
    n_row = len(refs) - 7
    pieces = refs[:n_row]
    send, keep, vals, panel, total, val_sems, piece_sems = refs[n_row:]
    core, row, live = place[0], place[1], count[0]
    blocks_here = pieces[0].shape[0]
    copies = []
    for step, piece in enumerate(pieces):
        owner = lax.rem(row + n_row - step, n_row)
        copies.append(
            pltpu.make_async_copy(
                piece, panel.at[pl.ds(owner * blocks_here, blocks_here)], piece_sems.at[step]
            )
        )
        copies[-1].start()
    start_chunks(live, vals_hbm, vals, val_sems, chunk)
    spare = total.shape[0] - 1

    def clear(block, unused):
        total[block] = jnp.zeros(total.shape[1:], F32)
        return unused

    lax.fori_loop(0, spare, clear, 0)
    for copy in copies:
        copy.wait()

    def one_slot(slot, alive):
        target = jnp.where(alive, rows[slot], spare)
        total[target] += jnp.dot(vals[slot], panel[cols[slot]], preferred_element_type=F32)

    each_live_slot(live, vals_hbm, vals, val_sems, chunk, one_slot)
    side, width = total.shape[1:]

    def split(chip, unused):
        first = 2 * blocks_here * chip
        other = total[pl.ds(first + blocks_here * (1 - core), blocks_here)]
        mine = total[pl.ds(first + blocks_here * core, blocks_here)]
        send[chip] = other.reshape(blocks_here * side, width).astype(BF16)
        keep[chip] = mine.reshape(blocks_here * side, width)
        return unused

    lax.fori_loop(0, send.shape[0], split, 0)


def backward_kernel(chunk, place, rows, cols, count, vals_hbm, same, other, out, vals, grads, total, val_sems, grad_sems):
    core, live = place[0], count[0]
    half = grads.shape[0] // 2
    copies = [
        pltpu.make_async_copy(same, grads.at[pl.ds(core * half, half)], grad_sems.at[0]),
        pltpu.make_async_copy(other, grads.at[pl.ds((1 - core) * half, half)], grad_sems.at[1]),
    ]
    for copy in copies:
        copy.start()
    start_chunks(live, vals_hbm, vals, val_sems, chunk)
    spare = total.shape[0] - 1
    for block in range(spare):
        total[block] = jnp.zeros(total.shape[1:], F32)
    for copy in copies:
        copy.wait()

    def one_slot(slot, alive):
        target = jnp.where(alive, cols[slot], spare)
        block = rows[slot]
        source = ((block >> 1) & 1) * half + (block >> 2) * 2 + (block & 1)
        total[target] += lax.dot_general(
            vals[slot], grads[source], (((0,), (0,)), ((), ())), preferred_element_type=F32
        )

    each_live_slot(live, vals_hbm, vals, val_sems, chunk, one_slot)
    for block in range(spare):
        out[block] = total[block].astype(BF16)


def dense_kernel(parts, weight, cotangent, activated, grad_agg, local_weight):
    total = parts[0].astype(F32)
    for chip in range(1, parts.shape[0]):
        total += parts[chip].astype(F32)
    aggregated = total.astype(BF16)
    pre = jnp.dot(aggregated, weight[...], preferred_element_type=F32)
    sigma = jax.nn.sigmoid(pre)
    activated[...] = (pre * sigma).astype(BF16)
    grad_pre = (cotangent[...].astype(F32) * sigma * (1.0 + pre * (1.0 - sigma))).astype(BF16)
    local_weight[...] = lax.dot_general(
        aggregated, grad_pre, (((0,), (0,)), ((), ())), preferred_element_type=F32
    )
    grad = lax.dot_general(
        grad_pre, weight[...], (((1,), (1,)), ((), ())), preferred_element_type=F32
    ).astype(BF16)
    for chip in range(grad_agg.shape[0]):
        grad_agg[chip] = grad


def per_device(features, weight, cotangent, blk_vals, blk_rows, blk_cols, blk_count):
    n_row, n_col = lax.axis_size("row"), lax.axis_size("col")
    nodes, width = cotangent.shape
    slots, side = blk_vals.shape[2], blk_vals.shape[3]
    here = nodes // side
    chips = n_col // 2
    chunk = slots // 8
    values = blk_vals[0, 0]
    place = jnp.stack([lax.axis_index("col") % 2, lax.axis_index("row")]).astype(jnp.int32)
    scalars = (place, blk_rows[0, 0], blk_cols[0, 0], blk_count[0])
    smem = pl.BlockSpec(memory_space=pltpu.SMEM)
    vmem = pl.BlockSpec(memory_space=pltpu.VMEM)
    hbm = pl.BlockSpec(memory_space=pl.ANY)
    swap = [(i, i ^ 1) for i in range(n_col)]
    same_core = [list(range(core, n_col, 2)) for core in range(2)]
    work = 2 * slots * side * side * width

    own = features.reshape(here, side, width)
    steps = [0] + sorted(range(1, n_row), key=lambda k: -min(k, n_row - k))
    moved = {0: own}
    for k in steps[1:]:
        moved[k] = lax.ppermute(own, "row", [(i, (i + k) % n_row) for i in range(n_row)])
    pieces = [moved[k] for k in range(n_row)]

    send, keep = pl.pallas_call(
        functools.partial(forward_kernel, chunk),
        out_shape=(
            jax.ShapeDtypeStruct((chips, nodes, width), BF16),
            jax.ShapeDtypeStruct((chips, nodes, width), F32),
        ),
        in_specs=[smem] * 4 + [hbm] * (1 + n_row),
        out_specs=(vmem, vmem),
        scratch_shapes=[
            pltpu.VMEM((slots, side, side), BF16),
            pltpu.VMEM((here * n_row, side, width), BF16),
            pltpu.VMEM((here * n_col + 1, side, width), F32),
            pltpu.SemaphoreType.DMA((slots // chunk,)),
            pltpu.SemaphoreType.DMA((n_row,)),
        ],
        compiler_params=pltpu.CompilerParams(vmem_limit_bytes=40 * MIB),
        cost_estimate=pl.CostEstimate(flops=work, bytes_accessed=14 * MIB, transcendentals=0),
    )(*scalars, values, *pieces)

    arrived = lax.ppermute(send, "col", swap)
    shares = (keep + arrived.astype(F32)).astype(BF16)
    parts = lax.all_to_all(shares, "col", 0, 0, tiled=True, axis_index_groups=same_core)

    activated, grad_agg, local_weight = pl.pallas_call(
        dense_kernel,
        out_shape=(
            jax.ShapeDtypeStruct((nodes, width), BF16),
            jax.ShapeDtypeStruct((chips, nodes, width), BF16),
            jax.ShapeDtypeStruct((width, width), F32),
        ),
        in_specs=[vmem] * 3,
        out_specs=(vmem,) * 3,
        compiler_params=pltpu.CompilerParams(vmem_limit_bytes=24 * MIB),
        cost_estimate=pl.CostEstimate(
            flops=6 * nodes * width * width, bytes_accessed=5 * MIB, transcendentals=nodes * width
        ),
    )(parts, weight, cotangent)

    same = lax.all_to_all(grad_agg, "col", 0, 0, tiled=True, axis_index_groups=same_core)
    other = lax.ppermute(same, "col", swap)

    strip = width // n_col
    terms = lax.all_to_all(local_weight.reshape(n_col, strip, width), "col", 0, 0, tiled=True)
    panel_sum = jnp.sum(terms, axis=0)
    copies = jnp.broadcast_to(panel_sum[None], (n_row, strip, width))
    strips = lax.all_to_all(copies, "row", 0, 0, tiled=True)
    strip_sum = jnp.sum(strips, axis=0)
    copies = jnp.broadcast_to(strip_sum[None], (n_col, strip, width))
    grad_weight = lax.all_to_all(copies, "col", 0, 0, tiled=True).reshape(width, width)

    blocks = chips * here
    partial_cols = pl.pallas_call(
        functools.partial(backward_kernel, chunk),
        out_shape=jax.ShapeDtypeStruct((here * n_row, side, width), BF16),
        in_specs=[smem] * 4 + [hbm] * 3,
        out_specs=vmem,
        scratch_shapes=[
            pltpu.VMEM((slots, side, side), BF16),
            pltpu.VMEM((2 * blocks, side, width), BF16),
            pltpu.VMEM((here * n_row + 1, side, width), F32),
            pltpu.SemaphoreType.DMA((slots // chunk,)),
            pltpu.SemaphoreType.DMA((2,)),
        ],
        compiler_params=pltpu.CompilerParams(vmem_limit_bytes=40 * MIB),
        cost_estimate=pl.CostEstimate(flops=work, bytes_accessed=11 * MIB, transcendentals=0),
    )(*scalars, values, same.reshape(blocks, side, width), other.reshape(blocks, side, width))

    own_cols = lax.all_to_all(
        partial_cols.reshape(n_row, nodes, width), "row", 0, 0, tiled=True
    )
    grad_features = jnp.sum(own_cols.astype(F32), axis=0).astype(BF16).reshape(1, nodes, width)
    return (activated, grad_weight, grad_features)


def solution(mesh):
    return jax.shard_map(
        per_device,
        mesh=mesh,
        in_specs=(
            P("col", "row", None),
            P(),
            P(("row", "col"), None),
            P("row", "col", None, None, None),
            P("row", "col", None),
            P("row", "col", None),
            P("row", "col"),
        ),
        out_specs=(P(("row", "col"), None), P(), P("col", "row", None)),
        check_vma=False,
    )
```

```python
import functools

import jax
import jax.numpy as jnp
from jax import lax
from jax.experimental import pallas as pl
from jax.experimental.pallas import tpu as pltpu
from jax.sharding import PartitionSpec as P

BF16 = jnp.bfloat16
F32 = jnp.float32
UNROLL = 16
MIB = 1 << 20


def start_chunks(live, vals_hbm, vals, sems, chunk):
    for piece in range(vals.shape[0] // chunk):

        @pl.when(piece * chunk < live)
        def _():
            part = pl.ds(piece * chunk, chunk)
            pltpu.make_async_copy(vals_hbm.at[part], vals.at[part], sems.at[piece]).start()


def each_live_slot(live, vals_hbm, vals, sems, chunk, one_slot):
    def one_chunk(piece, unused):
        part = pl.ds(piece * chunk, chunk)
        pltpu.make_async_copy(vals_hbm.at[part], vals.at[part], sems.at[piece]).wait()

        def one_group(group, unused):
            for lane in range(UNROLL):
                slot = piece * chunk + group * UNROLL + lane
                one_slot(slot, slot < live)
            return unused

        groups = (jnp.minimum(chunk, live - piece * chunk) + UNROLL - 1) // UNROLL
        return lax.fori_loop(0, groups, one_group, unused)

    lax.fori_loop(0, (live + chunk - 1) // chunk, one_chunk, 0)


def forward_kernel(chunk, place, rows, cols, count, vals_hbm, *refs):
    n_row = len(refs) - 7
    pieces = refs[:n_row]
    send, keep, vals, panel, total, val_sems, piece_sems = refs[n_row:]
    core, row, live = place[0], place[1], count[0]
    blocks_here = pieces[0].shape[0]
    copies = []
    for step, piece in enumerate(pieces):
        owner = lax.rem(row + n_row - step, n_row)
        copies.append(
            pltpu.make_async_copy(
                piece, panel.at[pl.ds(owner * blocks_here, blocks_here)], piece_sems.at[step]
            )
        )
        copies[-1].start()
    start_chunks(live, vals_hbm, vals, val_sems, chunk)
    spare = total.shape[0] - 1

    def clear(block, unused):
        total[block] = jnp.zeros(total.shape[1:], F32)
        return unused

    lax.fori_loop(0, spare, clear, 0)
    for copy in copies:
        copy.wait()

    def one_slot(slot, alive):
        target = jnp.where(alive, rows[slot], spare)
        total[target] += jnp.dot(vals[slot], panel[cols[slot]], preferred_element_type=F32)

    each_live_slot(live, vals_hbm, vals, val_sems, chunk, one_slot)
    side, width = total.shape[1:]

    def split(chip, unused):
        first = 2 * blocks_here * chip
        other = total[pl.ds(first + blocks_here * (1 - core), blocks_here)]
        mine = total[pl.ds(first + blocks_here * core, blocks_here)]
        send[chip] = other.reshape(blocks_here * side, width).astype(BF16)
        keep[chip] = mine.reshape(blocks_here * side, width)
        return unused

    lax.fori_loop(0, send.shape[0], split, 0)


def backward_kernel(chunk, place, rows, cols, count, vals_hbm, same, other, out, vals, grads, total, val_sems, grad_sems):
    core, live = place[0], count[0]
    side = total.shape[1]
    copies = [
        pltpu.make_async_copy(same, grads.at[core], grad_sems.at[0]),
        pltpu.make_async_copy(other, grads.at[1 - core], grad_sems.at[1]),
    ]
    for copy in copies:
        copy.start()
    start_chunks(live, vals_hbm, vals, val_sems, chunk)
    spare = total.shape[0] - 1
    for block in range(spare):
        total[block] = jnp.zeros(total.shape[1:], F32)
    for copy in copies:
        copy.wait()

    def one_slot(slot, alive):
        target = jnp.where(alive, cols[slot], spare)
        block = rows[slot]
        first = pl.multiple_of((block & 1) * side, side)
        picked = grads[(block >> 1) & 1, block >> 2, pl.ds(first, side)]
        total[target] += lax.dot_general(
            vals[slot], picked, (((0,), (0,)), ((), ())), preferred_element_type=F32
        )

    each_live_slot(live, vals_hbm, vals, val_sems, chunk, one_slot)
    for block in range(spare):
        out[block] = total[block].astype(BF16)


def dense_kernel(parts, weight, cotangent, activated, grad_agg):
    total = parts[0].astype(F32)
    for chip in range(1, parts.shape[0]):
        total += parts[chip].astype(F32)
    aggregated = total.astype(BF16)
    pre = jnp.dot(aggregated, weight[...], preferred_element_type=F32)
    sigma = jax.nn.sigmoid(pre)
    activated[...] = (pre * sigma).astype(BF16)
    grad_pre = (cotangent[...].astype(F32) * sigma * (1.0 + pre * (1.0 - sigma))).astype(BF16)
    local_weight = lax.dot_general(
        aggregated, grad_pre, (((0,), (0,)), ((), ())), preferred_element_type=F32
    ).astype(BF16)
    grad = lax.dot_general(
        grad_pre, weight[...], (((1,), (1,)), ((), ())), preferred_element_type=F32
    ).astype(BF16)
    nodes = grad.shape[0]
    strip = grad_agg.shape[1] - nodes
    for chip in range(grad_agg.shape[0]):
        grad_agg[chip, :nodes] = grad
        grad_agg[chip, nodes:] = local_weight[chip * strip : (chip + 1) * strip]


def per_device(features, weight, cotangent, blk_vals, blk_rows, blk_cols, blk_count):
    n_row, n_col = lax.axis_size("row"), lax.axis_size("col")
    nodes, width = cotangent.shape
    slots, side = blk_vals.shape[2], blk_vals.shape[3]
    here = nodes // side
    chips = n_col // 2
    chunk = slots // 6
    values = pltpu.with_memory_space_constraint(blk_vals[0, 0], pltpu.HBM)
    place = jnp.stack([lax.axis_index("col") % 2, lax.axis_index("row")]).astype(jnp.int32)
    scalars = (place, blk_rows[0, 0], blk_cols[0, 0], blk_count[0])
    smem = pl.BlockSpec(memory_space=pltpu.SMEM)
    vmem = pl.BlockSpec(memory_space=pltpu.VMEM)
    near = pl.BlockSpec(memory_space=pl.ANY)
    hbm = pl.BlockSpec(memory_space=pltpu.HBM)
    swap = [(i, i ^ 1) for i in range(n_col)]
    same_core = [list(range(core, n_col, 2)) for core in range(2)]
    work = 2 * slots * side * side * width

    own = features.reshape(here, side, width)
    steps = [0] + sorted(range(1, n_row), key=lambda k: -min(k, n_row - k))
    moved = {0: own}
    for k in steps[1:]:
        moved[k] = lax.ppermute(own, "row", [(i, (i + k) % n_row) for i in range(n_row)])
    pieces = [moved[k] for k in range(n_row)]

    send, keep = pl.pallas_call(
        functools.partial(forward_kernel, chunk),
        out_shape=(
            jax.ShapeDtypeStruct((chips, nodes, width), BF16),
            jax.ShapeDtypeStruct((chips, nodes, width), F32),
        ),
        in_specs=[smem] * 4 + [hbm] + [near] * n_row,
        out_specs=(vmem, vmem),
        scratch_shapes=[
            pltpu.VMEM((slots, side, side), BF16),
            pltpu.VMEM((here * n_row, side, width), BF16),
            pltpu.VMEM((here * n_col + 1, side, width), F32),
            pltpu.SemaphoreType.DMA((slots // chunk,)),
            pltpu.SemaphoreType.DMA((n_row,)),
        ],
        compiler_params=pltpu.CompilerParams(vmem_limit_bytes=40 * MIB),
        cost_estimate=pl.CostEstimate(flops=work, bytes_accessed=14 * MIB, transcendentals=0),
    )(*scalars, values, *pieces)

    arrived = lax.ppermute(send, "col", swap)
    shares = (keep + arrived.astype(F32)).astype(BF16)
    parts = lax.all_to_all(shares, "col", 0, 0, tiled=True, axis_index_groups=same_core)

    strip = width // chips
    activated, grad_agg = pl.pallas_call(
        dense_kernel,
        out_shape=(
            jax.ShapeDtypeStruct((nodes, width), BF16),
            jax.ShapeDtypeStruct((chips, nodes + strip, width), BF16),
        ),
        in_specs=[vmem] * 3,
        out_specs=(vmem,) * 2,
        compiler_params=pltpu.CompilerParams(vmem_limit_bytes=24 * MIB),
        cost_estimate=pl.CostEstimate(
            flops=6 * nodes * width * width, bytes_accessed=5 * MIB, transcendentals=nodes * width
        ),
    )(parts, weight, cotangent)

    same = lax.all_to_all(grad_agg, "col", 0, 0, tiled=True, axis_index_groups=same_core)
    other = lax.ppermute(same, "col", swap)

    terms = jnp.sum(same[:, nodes:].astype(F32), axis=0) + jnp.sum(other[:, nodes:].astype(F32), axis=0)
    half_strip = lax.dynamic_slice_in_dim(terms, place[0] * (strip // 2), strip // 2, 0)
    strips = lax.all_gather(half_strip, ("row", "col"), axis=0, tiled=True)
    grad_weight = jnp.sum(strips.reshape(n_row, width, width), axis=0)

    partial_cols = pl.pallas_call(
        functools.partial(backward_kernel, chunk),
        out_shape=jax.ShapeDtypeStruct((here * n_row, side, width), BF16),
        in_specs=[smem] * 4 + [hbm] + [near] * 2,
        out_specs=vmem,
        scratch_shapes=[
            pltpu.VMEM((slots, side, side), BF16),
            pltpu.VMEM((2, chips, nodes + strip, width), BF16),
            pltpu.VMEM((here * n_row + 1, side, width), F32),
            pltpu.SemaphoreType.DMA((slots // chunk,)),
            pltpu.SemaphoreType.DMA((2,)),
        ],
        compiler_params=pltpu.CompilerParams(vmem_limit_bytes=40 * MIB),
        cost_estimate=pl.CostEstimate(flops=work, bytes_accessed=11 * MIB, transcendentals=0),
    )(*scalars, values, same, other)

    own_cols = lax.all_to_all(
        partial_cols.reshape(n_row, nodes, width), "row", 0, 0, tiled=True
    )
    grad_features = jnp.sum(own_cols.astype(F32), axis=0).astype(BF16).reshape(1, nodes, width)
    return (activated, grad_weight, grad_features)


def solution(mesh):
    return jax.shard_map(
        per_device,
        mesh=mesh,
        in_specs=(
            P("col", "row", None),
            P(),
            P(("row", "col"), None),
            P("row", "col", None, None, None),
            P("row", "col", None),
            P("row", "col", None),
            P("row", "col"),
        ),
        out_specs=(P(("row", "col"), None), P(), P("col", "row", None)),
        check_vma=False,
    )
```

```python
import functools

import jax
import jax.numpy as jnp
from jax import lax
from jax.experimental import pallas as pl
from jax.experimental.pallas import tpu as pltpu
from jax.sharding import PartitionSpec as P

BF16 = jnp.bfloat16
F32 = jnp.float32
UNROLL = 32
MIB = 1 << 20


def start_chunks(live, vals_hbm, vals, sems, chunk):
    for piece in range(vals.shape[0] // chunk):

        @pl.when(piece * chunk < live)
        def _():
            part = pl.ds(piece * chunk, chunk)
            pltpu.make_async_copy(vals_hbm.at[part], vals.at[part], sems.at[piece]).start()


def each_live_slot(live, vals_hbm, vals, sems, chunk, one_slot):
    def one_chunk(piece, unused):
        part = pl.ds(piece * chunk, chunk)
        pltpu.make_async_copy(vals_hbm.at[part], vals.at[part], sems.at[piece]).wait()

        def one_group(group, unused):
            for lane in range(UNROLL):
                slot = piece * chunk + group * UNROLL + lane
                one_slot(slot, slot < live)
            return unused

        groups = (jnp.minimum(chunk, live - piece * chunk) + UNROLL - 1) // UNROLL
        return lax.fori_loop(0, groups, one_group, unused)

    lax.fori_loop(0, (live + chunk - 1) // chunk, one_chunk, 0)


def forward_kernel(chunk, steps, place, rows, cols, count, vals_hbm, *refs):
    n_row = len(refs) - 7
    pieces = refs[:n_row]
    send, keep, vals, panel, total, val_sems, piece_sems = refs[n_row:]
    core, row, live = place[0], place[1], count[0]
    blocks_here = pieces[0].shape[0]
    copies = []
    for at, (step, piece) in enumerate(zip(steps, pieces)):
        owner = lax.rem(row + n_row - step, n_row)
        copies.append(
            pltpu.make_async_copy(
                piece, panel.at[pl.ds(owner * blocks_here, blocks_here)], piece_sems.at[at]
            )
        )
        copies[-1].start()
    start_chunks(live, vals_hbm, vals, val_sems, chunk)
    spare = total.shape[0] - 1

    def clear(block, unused):
        total[block] = jnp.zeros(total.shape[1:], F32)
        return unused

    lax.fori_loop(0, spare, clear, 0)
    for copy in copies:
        copy.wait()

    def one_slot(slot, alive):
        target = jnp.where(alive, rows[slot], spare)
        total[target] += jnp.dot(vals[slot], panel[cols[slot]], preferred_element_type=F32)

    each_live_slot(live, vals_hbm, vals, val_sems, chunk, one_slot)
    side, width = total.shape[1:]

    def split(chip, unused):
        first = 2 * blocks_here * chip
        other = total[pl.ds(first + blocks_here * (1 - core), blocks_here)]
        mine = total[pl.ds(first + blocks_here * core, blocks_here)]
        send[chip] = other.reshape(blocks_here * side, width).astype(BF16)
        keep[chip] = mine.reshape(blocks_here * side, width)
        return unused

    lax.fori_loop(0, send.shape[0], split, 0)


def backward_kernel(chunk, steps, place, rows, cols, count, vals_hbm, same, other, *refs):
    n_row = len(steps)
    outs = refs[:n_row]
    vals, grads, total, val_sems, grad_sems = refs[n_row:]
    core, row, live = place[0], place[1], count[0]
    side = total.shape[1]
    copies = [
        pltpu.make_async_copy(same, grads.at[core], grad_sems.at[0]),
        pltpu.make_async_copy(other, grads.at[1 - core], grad_sems.at[1]),
    ]
    for copy in copies:
        copy.start()
    start_chunks(live, vals_hbm, vals, val_sems, chunk)
    spare = total.shape[0] - 1
    for block in range(spare):
        total[block] = jnp.zeros(total.shape[1:], F32)
    for copy in copies:
        copy.wait()

    def one_slot(slot, alive):
        target = jnp.where(alive, cols[slot], spare)
        block = rows[slot]
        first = pl.multiple_of((block & 1) * side, side)
        picked = grads[(block >> 1) & 1, block >> 2, pl.ds(first, side)]
        total[target] += lax.dot_general(
            vals[slot], picked, (((0,), (0,)), ((), ())), preferred_element_type=F32
        )

    each_live_slot(live, vals_hbm, vals, val_sems, chunk, one_slot)
    blocks_here = spare // n_row
    for step, out in zip(steps, outs):
        owner = lax.rem(row + step, n_row)
        mine = total[pl.ds(owner * blocks_here, blocks_here)]
        out[...] = mine.reshape(out.shape).astype(BF16)


def dense_kernel(parts, weight, cotangent, activated, grad_agg):
    total = parts[0].astype(F32)
    for chip in range(1, parts.shape[0]):
        total += parts[chip].astype(F32)
    aggregated = total.astype(BF16)
    pre = jnp.dot(aggregated, weight[...], preferred_element_type=F32)
    sigma = jax.nn.sigmoid(pre)
    activated[...] = (pre * sigma).astype(BF16)
    grad_pre = (cotangent[...].astype(F32) * sigma * (1.0 + pre * (1.0 - sigma))).astype(BF16)
    local_weight = lax.dot_general(
        aggregated, grad_pre, (((0,), (0,)), ((), ())), preferred_element_type=F32
    ).astype(BF16)
    grad = lax.dot_general(
        grad_pre, weight[...], (((1,), (1,)), ((), ())), preferred_element_type=F32
    ).astype(BF16)
    nodes = grad.shape[0]
    strip = grad_agg.shape[1] - nodes
    for chip in range(grad_agg.shape[0]):
        grad_agg[chip, :nodes] = grad
        grad_agg[chip, nodes:] = local_weight[chip * strip : (chip + 1) * strip]


def turn(size, step):
    return [(i, (i + step) % size) for i in range(size)]


def per_device(features, weight, cotangent, blk_vals, blk_rows, blk_cols, blk_count):
    n_row, n_col = lax.axis_size("row"), lax.axis_size("col")
    nodes, width = cotangent.shape
    slots, side = blk_vals.shape[2], blk_vals.shape[3]
    here = nodes // side
    chips = n_col // 2
    chunk = slots // 6
    values = pltpu.with_memory_space_constraint(blk_vals[0, 0], pltpu.HBM)
    place = jnp.stack([lax.axis_index("col") % 2, lax.axis_index("row")]).astype(jnp.int32)
    scalars = (place, blk_rows[0, 0], blk_cols[0, 0], blk_count[0])
    smem = pl.BlockSpec(memory_space=pltpu.SMEM)
    vmem = pl.BlockSpec(memory_space=pltpu.VMEM)
    near = pl.BlockSpec(memory_space=pl.ANY)
    hbm = pl.BlockSpec(memory_space=pltpu.HBM)
    swap = [(i, i ^ 1) for i in range(n_col)]
    same_core = [list(range(core, n_col, 2)) for core in range(2)]
    work = 2 * slots * side * side * width

    own = features.reshape(here, side, width)
    steps = [0] + sorted(range(1, n_row), key=lambda k: (-min(k, n_row - k), k))
    pieces = [own] + [lax.ppermute(own, "row", turn(n_row, k)) for k in steps[1:]]

    send, keep = pl.pallas_call(
        functools.partial(forward_kernel, chunk, steps),
        out_shape=(
            jax.ShapeDtypeStruct((chips, nodes, width), BF16),
            jax.ShapeDtypeStruct((chips, nodes, width), F32),
        ),
        in_specs=[smem] * 4 + [hbm] + [near] * n_row,
        out_specs=(vmem, vmem),
        scratch_shapes=[
            pltpu.VMEM((slots, side, side), BF16),
            pltpu.VMEM((here * n_row, side, width), BF16),
            pltpu.VMEM((here * n_col + 1, side, width), F32),
            pltpu.SemaphoreType.DMA((slots // chunk,)),
            pltpu.SemaphoreType.DMA((n_row,)),
        ],
        compiler_params=pltpu.CompilerParams(vmem_limit_bytes=40 * MIB),
        cost_estimate=pl.CostEstimate(flops=work, bytes_accessed=14 * MIB, transcendentals=0),
    )(*scalars, values, *pieces)

    arrived = lax.ppermute(send, "col", swap)
    shares = (keep + arrived.astype(F32)).astype(BF16)
    parts = lax.all_to_all(shares, "col", 0, 0, tiled=True, axis_index_groups=same_core)

    strip = width // chips
    activated, grad_agg = pl.pallas_call(
        dense_kernel,
        out_shape=(
            jax.ShapeDtypeStruct((nodes, width), BF16),
            jax.ShapeDtypeStruct((chips, nodes + strip, width), BF16),
        ),
        in_specs=[vmem] * 3,
        out_specs=(vmem,) * 2,
        compiler_params=pltpu.CompilerParams(vmem_limit_bytes=24 * MIB),
        cost_estimate=pl.CostEstimate(
            flops=6 * nodes * width * width, bytes_accessed=5 * MIB, transcendentals=nodes * width
        ),
    )(parts, weight, cotangent)

    same = lax.all_to_all(grad_agg, "col", 0, 0, tiled=True, axis_index_groups=same_core)
    other = lax.ppermute(same, "col", swap)

    terms = jnp.sum(same[:, nodes:].astype(F32), axis=0) + jnp.sum(other[:, nodes:].astype(F32), axis=0)
    rows_core = strip // 2
    half_strip = lax.dynamic_slice_in_dim(terms, place[0] * rows_core, rows_core, 0)
    copies = jnp.broadcast_to(half_strip[None], (n_row, rows_core, width))
    strips = lax.all_to_all(copies, "row", 0, 0, tiled=True)
    copies = jnp.broadcast_to(jnp.sum(strips, axis=0)[None], (n_col, rows_core, width))
    grad_weight = lax.all_to_all(copies, "col", 0, 0, tiled=True).reshape(width, width)

    shares = pl.pallas_call(
        functools.partial(backward_kernel, chunk, steps),
        out_shape=(jax.ShapeDtypeStruct((nodes, width), BF16),) * n_row,
        in_specs=[smem] * 4 + [hbm] + [near] * 2,
        out_specs=(vmem,) * n_row,
        scratch_shapes=[
            pltpu.VMEM((slots, side, side), BF16),
            pltpu.VMEM((2, chips, nodes + strip, width), BF16),
            pltpu.VMEM((here * n_row + 1, side, width), F32),
            pltpu.SemaphoreType.DMA((slots // chunk,)),
            pltpu.SemaphoreType.DMA((2,)),
        ],
        compiler_params=pltpu.CompilerParams(vmem_limit_bytes=40 * MIB),
        cost_estimate=pl.CostEstimate(flops=work, bytes_accessed=11 * MIB, transcendentals=0),
    )(*scalars, values, same, other)

    total = shares[0].astype(F32)
    for step, share in zip(steps[1:], shares[1:]):
        total += lax.ppermute(share, "row", turn(n_row, step)).astype(F32)
    grad_features = total.astype(BF16).reshape(1, nodes, width)
    return (activated, grad_weight, grad_features)


def solution(mesh):
    return jax.shard_map(
        per_device,
        mesh=mesh,
        in_specs=(
            P("col", "row", None),
            P(),
            P(("row", "col"), None),
            P("row", "col", None, None, None),
            P("row", "col", None),
            P("row", "col", None),
            P("row", "col"),
        ),
        out_specs=(P(("row", "col"), None), P(), P("col", "row", None)),
        check_vma=False,
    )
```

```python
import functools

import jax
import jax.numpy as jnp
from jax import lax
from jax.experimental import pallas as pl
from jax.experimental.pallas import tpu as pltpu
from jax.sharding import PartitionSpec as P

BF16 = jnp.bfloat16
F32 = jnp.float32
UNROLL = 32
MIB = 1 << 20


def start_chunks(live, vals_hbm, vals, sems, chunk):
    for piece in range(vals.shape[0] // chunk):

        @pl.when(piece * chunk < live)
        def _():
            part = pl.ds(piece * chunk, chunk)
            pltpu.make_async_copy(vals_hbm.at[part], vals.at[part], sems.at[piece]).start()


def each_live_slot(live, vals_hbm, vals, sems, chunk, one_slot):
    def one_chunk(piece, unused):
        part = pl.ds(piece * chunk, chunk)
        pltpu.make_async_copy(vals_hbm.at[part], vals.at[part], sems.at[piece]).wait()

        def one_group(group, unused):
            for lane in range(UNROLL):
                slot = piece * chunk + group * UNROLL + lane
                one_slot(slot, slot < live)
            return unused

        groups = (jnp.minimum(chunk, live - piece * chunk) + UNROLL - 1) // UNROLL
        return lax.fori_loop(0, groups, one_group, unused)

    lax.fori_loop(0, (live + chunk - 1) // chunk, one_chunk, 0)


def forward_kernel(chunk, steps, place, rows, cols, count, vals_hbm, *refs):
    n_row = len(refs) - 7
    pieces = refs[:n_row]
    send, keep, vals, panel, total, val_sems, piece_sems = refs[n_row:]
    core, row, live = place[0], place[1], count[0]
    blocks_here = pieces[0].shape[0]
    copies = []
    for at, (step, piece) in enumerate(zip(steps, pieces)):
        owner = lax.rem(row + n_row - step, n_row)
        copies.append(
            pltpu.make_async_copy(
                piece, panel.at[pl.ds(owner * blocks_here, blocks_here)], piece_sems.at[at]
            )
        )
        copies[-1].start()
    start_chunks(live, vals_hbm, vals, val_sems, chunk)
    spare = total.shape[0] - 1

    def clear(block, unused):
        total[block] = jnp.zeros(total.shape[1:], F32)
        return unused

    lax.fori_loop(0, spare, clear, 0)
    for copy in copies:
        copy.wait()

    def one_slot(slot, alive):
        target = jnp.where(alive, rows[slot], spare)
        total[target] += jnp.dot(vals[slot], panel[cols[slot]], preferred_element_type=F32)

    each_live_slot(live, vals_hbm, vals, val_sems, chunk, one_slot)
    side, width = total.shape[1:]

    def split(chip, unused):
        first = 2 * blocks_here * chip
        other = total[pl.ds(first + blocks_here * (1 - core), blocks_here)]
        mine = total[pl.ds(first + blocks_here * core, blocks_here)]
        send[chip] = other.reshape(blocks_here * side, width).astype(BF16)
        keep[chip] = mine.reshape(blocks_here * side, width)
        return unused

    lax.fori_loop(0, send.shape[0], split, 0)


def backward_kernel(chunk, steps, place, rows, cols, count, vals_hbm, same, other, *refs):
    n_row = len(steps)
    outs = refs[:n_row]
    vals, grads, total, val_sems, grad_sems = refs[n_row:]
    core, row, live = place[0], place[1], count[0]
    side = total.shape[1]
    copies = [
        pltpu.make_async_copy(same, grads.at[core], grad_sems.at[0]),
        pltpu.make_async_copy(other, grads.at[1 - core], grad_sems.at[1]),
    ]
    for copy in copies:
        copy.start()
    start_chunks(live, vals_hbm, vals, val_sems, chunk)
    spare = total.shape[0] - 1
    for block in range(spare):
        total[block] = jnp.zeros(total.shape[1:], F32)
    for copy in copies:
        copy.wait()

    def one_slot(slot, alive):
        target = jnp.where(alive, cols[slot], spare)
        block = rows[slot]
        first = pl.multiple_of((block & 1) * side, side)
        picked = grads[(block >> 1) & 1, block >> 2, pl.ds(first, side)]
        total[target] += lax.dot_general(
            vals[slot], picked, (((0,), (0,)), ((), ())), preferred_element_type=F32
        )

    each_live_slot(live, vals_hbm, vals, val_sems, chunk, one_slot)
    blocks_here = spare // n_row
    for step, out in zip(steps, outs):
        owner = lax.rem(row + step, n_row)
        mine = total[pl.ds(owner * blocks_here, blocks_here)]
        out[...] = mine.reshape(out.shape).astype(BF16)


def dense_kernel(parts, weight, cotangent, activated, grad_agg):
    total = parts[0].astype(F32)
    for chip in range(1, parts.shape[0]):
        total += parts[chip].astype(F32)
    aggregated = total.astype(BF16)
    pre = jnp.dot(aggregated, weight[...], preferred_element_type=F32)
    sigma = jax.nn.sigmoid(pre)
    activated[...] = (pre * sigma).astype(BF16)
    grad_pre = (cotangent[...].astype(F32) * sigma * (1.0 + pre * (1.0 - sigma))).astype(BF16)
    local_weight = lax.dot_general(
        aggregated, grad_pre, (((0,), (0,)), ((), ())), preferred_element_type=F32
    ).astype(BF16)
    grad = lax.dot_general(
        grad_pre, weight[...], (((1,), (1,)), ((), ())), preferred_element_type=F32
    ).astype(BF16)
    nodes = grad.shape[0]
    strip = grad_agg.shape[1] - nodes
    for chip in range(grad_agg.shape[0]):
        grad_agg[chip, :nodes] = grad
        grad_agg[chip, nodes:] = local_weight[chip * strip : (chip + 1) * strip]


def turn(size, step):
    return [(i, (i + step) % size) for i in range(size)]


def per_device(features, weight, cotangent, blk_vals, blk_rows, blk_cols, blk_count):
    n_row, n_col = lax.axis_size("row"), lax.axis_size("col")
    nodes, width = cotangent.shape
    slots, side = blk_vals.shape[2], blk_vals.shape[3]
    here = nodes // side
    chips = n_col // 2
    chunk = slots // 6
    values = pltpu.with_memory_space_constraint(blk_vals[0, 0], pltpu.HBM)
    place = jnp.stack([lax.axis_index("col") % 2, lax.axis_index("row")]).astype(jnp.int32)
    scalars = (place, blk_rows[0, 0], blk_cols[0, 0], blk_count[0])
    smem = pl.BlockSpec(memory_space=pltpu.SMEM)
    vmem = pl.BlockSpec(memory_space=pltpu.VMEM)
    near = pl.BlockSpec(memory_space=pl.ANY)
    hbm = pl.BlockSpec(memory_space=pltpu.HBM)
    swap = [(i, i ^ 1) for i in range(n_col)]
    same_core = [list(range(core, n_col, 2)) for core in range(2)]
    work = 2 * slots * side * side * width

    own = features.reshape(here, side, width)
    steps = [0] + sorted(range(1, n_row), key=lambda k: (-min(k, n_row - k), k))
    pieces = [own] + [lax.ppermute(own, "row", turn(n_row, k)) for k in steps[1:]]

    send, keep = pl.pallas_call(
        functools.partial(forward_kernel, chunk, steps),
        out_shape=(
            jax.ShapeDtypeStruct((chips, nodes, width), BF16),
            jax.ShapeDtypeStruct((chips, nodes, width), F32),
        ),
        in_specs=[smem] * 4 + [hbm] + [near] * n_row,
        out_specs=(vmem, vmem),
        scratch_shapes=[
            pltpu.VMEM((slots, side, side), BF16),
            pltpu.VMEM((here * n_row, side, width), BF16),
            pltpu.VMEM((here * n_col + 1, side, width), F32),
            pltpu.SemaphoreType.DMA((slots // chunk,)),
            pltpu.SemaphoreType.DMA((n_row,)),
        ],
        compiler_params=pltpu.CompilerParams(vmem_limit_bytes=40 * MIB),
        cost_estimate=pl.CostEstimate(flops=work, bytes_accessed=14 * MIB, transcendentals=0),
    )(*scalars, values, *pieces)

    arrived = lax.ppermute(send, "col", swap)
    shares = (keep + arrived.astype(F32)).astype(BF16)
    parts = lax.all_to_all(shares, "col", 0, 0, tiled=True, axis_index_groups=same_core)

    strip = width // chips
    activated, grad_agg = pl.pallas_call(
        dense_kernel,
        out_shape=(
            jax.ShapeDtypeStruct((nodes, width), BF16),
            jax.ShapeDtypeStruct((chips, nodes + strip, width), BF16),
        ),
        in_specs=[vmem] * 3,
        out_specs=(vmem,) * 2,
        compiler_params=pltpu.CompilerParams(vmem_limit_bytes=24 * MIB),
        cost_estimate=pl.CostEstimate(
            flops=6 * nodes * width * width, bytes_accessed=5 * MIB, transcendentals=nodes * width
        ),
    )(parts, weight, cotangent)

    same = lax.all_to_all(grad_agg, "col", 0, 0, tiled=True, axis_index_groups=same_core)
    other = lax.ppermute(same, "col", swap)

    terms = jnp.sum(same[:, nodes:].astype(F32), axis=0) + jnp.sum(other[:, nodes:].astype(F32), axis=0)
    rows_core = strip // 2
    half_strip = lax.dynamic_slice_in_dim(terms, place[0] * rows_core, rows_core, 0)
    copies = jnp.broadcast_to(half_strip[None], (n_row, rows_core, width))
    strips = lax.all_to_all(copies, "row", 0, 0, tiled=True)
    copies = jnp.broadcast_to(jnp.sum(strips, axis=0)[None], (n_col, rows_core, width))

    shares = pl.pallas_call(
        functools.partial(backward_kernel, chunk, steps),
        out_shape=(jax.ShapeDtypeStruct((nodes, width), BF16),) * n_row,
        in_specs=[smem] * 4 + [hbm] + [near] * 2,
        out_specs=(vmem,) * n_row,
        scratch_shapes=[
            pltpu.VMEM((slots, side, side), BF16),
            pltpu.VMEM((2, chips, nodes + strip, width), BF16),
            pltpu.VMEM((here * n_row + 1, side, width), F32),
            pltpu.SemaphoreType.DMA((slots // chunk,)),
            pltpu.SemaphoreType.DMA((2,)),
        ],
        compiler_params=pltpu.CompilerParams(vmem_limit_bytes=40 * MIB),
        cost_estimate=pl.CostEstimate(flops=work, bytes_accessed=11 * MIB, transcendentals=0),
    )(*scalars, values, same, other)

    shares, copies = lax.optimization_barrier((shares, copies))
    grad_weight = lax.all_to_all(copies, "col", 0, 0, tiled=True).reshape(width, width)
    total = shares[0].astype(F32)
    for step, share in zip(steps[1:], shares[1:]):
        total += lax.ppermute(share, "row", turn(n_row, step)).astype(F32)
    grad_features = total.astype(BF16).reshape(1, nodes, width)
    return (activated, grad_weight, grad_features)


def solution(mesh):
    return jax.shard_map(
        per_device,
        mesh=mesh,
        in_specs=(
            P("col", "row", None),
            P(),
            P(("row", "col"), None),
            P("row", "col", None, None, None),
            P("row", "col", None),
            P("row", "col", None),
            P("row", "col"),
        ),
        out_specs=(P(("row", "col"), None), P(), P("col", "row", None)),
        check_vma=False,
    )
```

```python
import functools

import jax
import jax.numpy as jnp
from jax import lax
from jax.experimental import pallas as pl
from jax.experimental.pallas import tpu as pltpu
from jax.sharding import PartitionSpec as P

BF16 = jnp.bfloat16
F32 = jnp.float32
UNROLL = 32
MIB = 1 << 20


def start_lists(sources, targets, sems):
    copies = [
        pltpu.make_async_copy(source, target, sems.at[at])
        for at, (source, target) in enumerate(zip(sources, targets))
    ]
    for copy in copies:
        copy.start()
    return copies


def start_chunks(live, vals_hbm, vals, sems, chunk):
    for piece in range(vals.shape[0] // chunk):

        @pl.when(piece * chunk < live)
        def _():
            part = pl.ds(piece * chunk, chunk)
            pltpu.make_async_copy(vals_hbm.at[part], vals.at[part], sems.at[piece]).start()


def each_live_slot(live, vals_hbm, vals, sems, chunk, one_slot):
    def one_chunk(piece, unused):
        part = pl.ds(piece * chunk, chunk)
        pltpu.make_async_copy(vals_hbm.at[part], vals.at[part], sems.at[piece]).wait()

        def one_group(group, unused):
            for lane in range(UNROLL):
                slot = piece * chunk + group * UNROLL + lane
                one_slot(slot, slot < live)
            return unused

        groups = (jnp.minimum(chunk, live - piece * chunk) + UNROLL - 1) // UNROLL
        return lax.fori_loop(0, groups, one_group, unused)

    lax.fori_loop(0, (live + chunk - 1) // chunk, one_chunk, 0)


def forward_kernel(chunk, steps, place, count, rows_hbm, cols_hbm, vals_hbm, *refs):
    n_row = len(refs) - 10
    pieces = refs[:n_row]
    send, keep, rows, cols, vals, panel, total, index_sems, val_sems, piece_sems = refs[n_row:]
    core, row, live = place[0], place[1], count[0]
    blocks_here = pieces[0].shape[0]
    copies = start_lists((rows_hbm, cols_hbm), (rows, cols), index_sems)
    for at, (step, piece) in enumerate(zip(steps, pieces)):
        owner = lax.rem(row + n_row - step, n_row)
        copies.append(
            pltpu.make_async_copy(
                piece, panel.at[pl.ds(owner * blocks_here, blocks_here)], piece_sems.at[at]
            )
        )
        copies[-1].start()
    start_chunks(live, vals_hbm, vals, val_sems, chunk)
    spare = total.shape[0] - 1

    def clear(block, unused):
        total[block] = jnp.zeros(total.shape[1:], F32)
        return unused

    lax.fori_loop(0, spare, clear, 0)
    for copy in copies:
        copy.wait()

    def one_slot(slot, alive):
        target = jnp.where(alive, rows[slot], spare)
        total[target] += jnp.dot(vals[slot], panel[cols[slot]], preferred_element_type=F32)

    each_live_slot(live, vals_hbm, vals, val_sems, chunk, one_slot)
    side, width = total.shape[1:]

    def split(chip, unused):
        first = 2 * blocks_here * chip
        other = total[pl.ds(first + blocks_here * (1 - core), blocks_here)]
        mine = total[pl.ds(first + blocks_here * core, blocks_here)]
        send[chip] = other.reshape(blocks_here * side, width).astype(BF16)
        keep[chip] = mine.reshape(blocks_here * side, width)
        return unused

    lax.fori_loop(0, send.shape[0], split, 0)


def backward_kernel(chunk, steps, place, count, rows_hbm, cols_hbm, vals_hbm, same, other, *refs):
    n_row = len(steps)
    outs = refs[:n_row]
    rows, cols, vals, grads, total, index_sems, val_sems, grad_sems = refs[n_row:]
    core, row, live = place[0], place[1], count[0]
    side = total.shape[1]
    copies = [
        pltpu.make_async_copy(same, grads.at[core], grad_sems.at[0]),
        pltpu.make_async_copy(other, grads.at[1 - core], grad_sems.at[1]),
    ]
    for copy in copies:
        copy.start()
    copies += start_lists((rows_hbm, cols_hbm), (rows, cols), index_sems)
    start_chunks(live, vals_hbm, vals, val_sems, chunk)
    spare = total.shape[0] - 1
    for block in range(spare):
        total[block] = jnp.zeros(total.shape[1:], F32)
    for copy in copies:
        copy.wait()

    def one_slot(slot, alive):
        target = jnp.where(alive, cols[slot], spare)
        block = rows[slot]
        first = pl.multiple_of((block & 1) * side, side)
        picked = grads[(block >> 1) & 1, block >> 2, pl.ds(first, side)]
        total[target] += lax.dot_general(
            vals[slot], picked, (((0,), (0,)), ((), ())), preferred_element_type=F32
        )

    each_live_slot(live, vals_hbm, vals, val_sems, chunk, one_slot)
    blocks_here = spare // n_row
    nodes = blocks_here * side
    terms = jnp.sum(grads[0, :, nodes:].astype(F32), axis=0) + jnp.sum(
        grads[1, :, nodes:].astype(F32), axis=0
    )
    half = terms.shape[0] // 2
    terms = jnp.where(core == 0, terms[:half], terms[half:])
    high = terms.astype(BF16).astype(F32)
    tail = jnp.concatenate([high, terms - high], axis=0).astype(BF16)
    for step, out in zip(steps, outs):
        owner = lax.rem(row + step, n_row)
        mine = total[pl.ds(owner * blocks_here, blocks_here)]
        out[:nodes] = mine.reshape(nodes, out.shape[1]).astype(BF16)
        out[nodes:] = tail


def copy_kernel(source, target, sem):
    copy = pltpu.make_async_copy(source, target, sem)
    copy.start()
    copy.wait()


def dense_kernel(parts, weight, cotangent, activated, grad_agg):
    total = parts[0].astype(F32)
    for chip in range(1, parts.shape[0]):
        total += parts[chip].astype(F32)
    aggregated = total.astype(BF16)
    pre = jnp.dot(aggregated, weight[...], preferred_element_type=F32)
    sigma = jax.nn.sigmoid(pre)
    activated[...] = (pre * sigma).astype(BF16)
    grad_pre = (cotangent[...].astype(F32) * sigma * (1.0 + pre * (1.0 - sigma))).astype(BF16)
    local_weight = lax.dot_general(
        aggregated, grad_pre, (((0,), (0,)), ((), ())), preferred_element_type=F32
    ).astype(BF16)
    grad = lax.dot_general(
        grad_pre, weight[...], (((1,), (1,)), ((), ())), preferred_element_type=F32
    ).astype(BF16)
    nodes = grad.shape[0]
    strip = grad_agg.shape[1] - nodes
    for chip in range(grad_agg.shape[0]):
        grad_agg[chip, :nodes] = grad
        grad_agg[chip, nodes:] = local_weight[chip * strip : (chip + 1) * strip]


def turn(size, step):
    return [(i, (i + step) % size) for i in range(size)]


def per_device(features, weight, cotangent, blk_vals, blk_rows, blk_cols, blk_count):
    n_row, n_col = lax.axis_size("row"), lax.axis_size("col")
    nodes, width = cotangent.shape
    slots, side = blk_vals.shape[2], blk_vals.shape[3]
    here = nodes // side
    chips = n_col // 2
    chunk = slots // 6
    place = jnp.stack([lax.axis_index("col") % 2, lax.axis_index("row")]).astype(jnp.int32)
    in_hbm = functools.partial(pltpu.with_memory_space_constraint, memory_space=pltpu.HBM)
    scalars = (place, blk_count[0], in_hbm(blk_rows[0, 0]), in_hbm(blk_cols[0, 0]))
    values = in_hbm(blk_vals[0, 0])
    smem = pl.BlockSpec(memory_space=pltpu.SMEM)
    vmem = pl.BlockSpec(memory_space=pltpu.VMEM)
    near = pl.BlockSpec(memory_space=pl.ANY)
    hbm = pl.BlockSpec(memory_space=pltpu.HBM)
    swap = [(i, i ^ 1) for i in range(n_col)]
    same_core = [list(range(core, n_col, 2)) for core in range(2)]
    work = 2 * slots * side * side * width

    own = pl.pallas_call(
        copy_kernel,
        out_shape=jax.ShapeDtypeStruct((here, side, width), BF16),
        in_specs=[hbm],
        out_specs=vmem,
        scratch_shapes=[pltpu.SemaphoreType.DMA],
        compiler_params=pltpu.CompilerParams(vmem_limit_bytes=4 * MIB),
    )(in_hbm(features.reshape(here, side, width)))
    steps = [0] + sorted(range(1, n_row), key=lambda k: (-min(k, n_row - k), k))
    pieces = [own] + [lax.ppermute(own, "row", turn(n_row, k)) for k in steps[1:]]

    send, keep = pl.pallas_call(
        functools.partial(forward_kernel, chunk, steps),
        out_shape=(
            jax.ShapeDtypeStruct((chips, nodes, width), BF16),
            jax.ShapeDtypeStruct((chips, nodes, width), F32),
        ),
        in_specs=[smem] * 2 + [hbm] * 3 + [near] * n_row,
        out_specs=(vmem, vmem),
        scratch_shapes=[
            pltpu.SMEM((slots,), jnp.int32),
            pltpu.SMEM((slots,), jnp.int32),
            pltpu.VMEM((slots, side, side), BF16),
            pltpu.VMEM((here * n_row, side, width), BF16),
            pltpu.VMEM((here * n_col + 1, side, width), F32),
            pltpu.SemaphoreType.DMA((2,)),
            pltpu.SemaphoreType.DMA((slots // chunk,)),
            pltpu.SemaphoreType.DMA((n_row,)),
        ],
        compiler_params=pltpu.CompilerParams(vmem_limit_bytes=40 * MIB),
        cost_estimate=pl.CostEstimate(flops=work, bytes_accessed=14 * MIB, transcendentals=0),
    )(*scalars, values, *pieces)

    arrived = lax.ppermute(send, "col", swap)
    shares = (keep + arrived.astype(F32)).astype(BF16)
    parts = lax.all_to_all(shares, "col", 0, 0, tiled=True, axis_index_groups=same_core)

    strip = width // chips
    activated, grad_agg = pl.pallas_call(
        dense_kernel,
        out_shape=(
            jax.ShapeDtypeStruct((nodes, width), BF16),
            jax.ShapeDtypeStruct((chips, nodes + strip, width), BF16),
        ),
        in_specs=[vmem] * 3,
        out_specs=(vmem,) * 2,
        compiler_params=pltpu.CompilerParams(vmem_limit_bytes=24 * MIB),
        cost_estimate=pl.CostEstimate(
            flops=6 * nodes * width * width, bytes_accessed=5 * MIB, transcendentals=nodes * width
        ),
    )(parts, weight, cotangent)

    same = lax.all_to_all(grad_agg, "col", 0, 0, tiled=True, axis_index_groups=same_core)
    other = lax.ppermute(same, "col", swap)

    shares = pl.pallas_call(
        functools.partial(backward_kernel, chunk, steps),
        out_shape=(jax.ShapeDtypeStruct((nodes + strip, width), BF16),) * n_row,
        in_specs=[smem] * 2 + [hbm] * 3 + [near] * 2,
        out_specs=(vmem,) * n_row,
        scratch_shapes=[
            pltpu.SMEM((slots,), jnp.int32),
            pltpu.SMEM((slots,), jnp.int32),
            pltpu.VMEM((slots, side, side), BF16),
            pltpu.VMEM((2, chips, nodes + strip, width), BF16),
            pltpu.VMEM((here * n_row + 1, side, width), F32),
            pltpu.SemaphoreType.DMA((2,)),
            pltpu.SemaphoreType.DMA((slots // chunk,)),
            pltpu.SemaphoreType.DMA((2,)),
        ],
        compiler_params=pltpu.CompilerParams(vmem_limit_bytes=40 * MIB),
        cost_estimate=pl.CostEstimate(flops=work, bytes_accessed=11 * MIB, transcendentals=0),
    )(*scalars, values, same, other)

    total = shares[0].astype(F32)
    for step, share in zip(steps[1:], shares[1:]):
        total += lax.ppermute(share, "row", turn(n_row, step)).astype(F32)
    grad_features = total[:nodes].astype(BF16).reshape(1, nodes, width)
    high, low = total[nodes : nodes + strip // 2], total[nodes + strip // 2 :]
    copies = jnp.broadcast_to((high + low)[None], (n_col, strip // 2, width))
    grad_weight = lax.all_to_all(copies, "col", 0, 0, tiled=True).reshape(width, width)
    return (activated, grad_weight, grad_features)


def solution(mesh):
    return jax.shard_map(
        per_device,
        mesh=mesh,
        in_specs=(
            P("col", "row", None),
            P(),
            P(("row", "col"), None),
            P("row", "col", None, None, None),
            P("row", "col", None),
            P("row", "col", None),
            P("row", "col"),
        ),
        out_specs=(P(("row", "col"), None), P(), P("col", "row", None)),
        check_vma=False,
    )
```

```python
import functools

import jax
import jax.numpy as jnp
from jax import lax
from jax.experimental import pallas as pl
from jax.experimental.pallas import tpu as pltpu
from jax.sharding import PartitionSpec as P

BF16 = jnp.bfloat16
F32 = jnp.float32
UNROLL = 32
MIB = 1 << 20


def start_lists(sources, targets, sems):
    copies = [
        pltpu.make_async_copy(source, target, sems.at[at])
        for at, (source, target) in enumerate(zip(sources, targets))
    ]
    for copy in copies:
        copy.start()
    return copies


def start_chunks(live, vals_hbm, vals, sems, chunk):
    for piece in range(vals.shape[0] // chunk):

        @pl.when(piece * chunk < live)
        def _():
            part = pl.ds(piece * chunk, chunk)
            pltpu.make_async_copy(vals_hbm.at[part], vals.at[part], sems.at[piece]).start()


def each_live_slot(live, vals_hbm, vals, sems, chunk, one_slot):
    def one_chunk(piece, unused):
        part = pl.ds(piece * chunk, chunk)
        pltpu.make_async_copy(vals_hbm.at[part], vals.at[part], sems.at[piece]).wait()

        def one_group(group, unused):
            for lane in range(UNROLL):
                slot = piece * chunk + group * UNROLL + lane
                one_slot(slot, slot < live)
            return unused

        groups = (jnp.minimum(chunk, live - piece * chunk) + UNROLL - 1) // UNROLL
        return lax.fori_loop(0, groups, one_group, unused)

    lax.fori_loop(0, (live + chunk - 1) // chunk, one_chunk, 0)


def forward_kernel(chunk, steps, place, count, rows_hbm, cols_hbm, vals_hbm, *refs):
    n_row = len(refs) - 10
    pieces = refs[:n_row]
    send, keep, rows, cols, vals, panel, total, index_sems, val_sems, piece_sems = refs[n_row:]
    core, row, live = place[0], place[1], count[0]
    blocks_here = pieces[0].shape[0]
    copies = start_lists((rows_hbm, cols_hbm), (rows, cols), index_sems)
    for at, (step, piece) in enumerate(zip(steps, pieces)):
        owner = lax.rem(row + n_row - step, n_row)
        copies.append(
            pltpu.make_async_copy(
                piece, panel.at[pl.ds(owner * blocks_here, blocks_here)], piece_sems.at[at]
            )
        )
        copies[-1].start()
    start_chunks(live, vals_hbm, vals, val_sems, chunk)
    spare = total.shape[0] - 1

    def clear(block, unused):
        total[block] = jnp.zeros(total.shape[1:], F32)
        return unused

    lax.fori_loop(0, spare, clear, 0)
    for copy in copies:
        copy.wait()

    def one_slot(slot, alive):
        target = jnp.where(alive, rows[slot], spare)
        total[target] += jnp.dot(vals[slot], panel[cols[slot]], preferred_element_type=F32)

    each_live_slot(live, vals_hbm, vals, val_sems, chunk, one_slot)
    side, width = total.shape[1:]

    def split(chip, unused):
        first = 2 * blocks_here * chip
        other = total[pl.ds(first + blocks_here * (1 - core), blocks_here)]
        mine = total[pl.ds(first + blocks_here * core, blocks_here)]
        send[chip] = other.reshape(blocks_here * side, width).astype(BF16)
        keep[chip] = mine.reshape(blocks_here * side, width)
        return unused

    lax.fori_loop(0, send.shape[0], split, 0)


def backward_kernel(chunk, steps, place, count, rows_hbm, cols_hbm, vals_hbm, same, other, *refs):
    n_row = len(steps)
    outs = refs[:n_row]
    rows, cols, vals, grads, total, index_sems, val_sems, grad_sems = refs[n_row:]
    core, row, live = place[0], place[1], count[0]
    side = total.shape[1]
    copies = [
        pltpu.make_async_copy(same, grads.at[core], grad_sems.at[0]),
        pltpu.make_async_copy(other, grads.at[1 - core], grad_sems.at[1]),
    ]
    for copy in copies:
        copy.start()
    copies += start_lists((rows_hbm, cols_hbm), (rows, cols), index_sems)
    start_chunks(live, vals_hbm, vals, val_sems, chunk)
    spare = total.shape[0] - 1
    for block in range(spare):
        total[block] = jnp.zeros(total.shape[1:], F32)
    for copy in copies:
        copy.wait()

    def one_slot(slot, alive):
        target = jnp.where(alive, cols[slot], spare)
        block = rows[slot]
        first = pl.multiple_of((block & 1) * side, side)
        picked = grads[(block >> 1) & 1, block >> 2, pl.ds(first, side)]
        total[target] += lax.dot_general(
            vals[slot], picked, (((0,), (0,)), ((), ())), preferred_element_type=F32
        )

    each_live_slot(live, vals_hbm, vals, val_sems, chunk, one_slot)
    blocks_here = spare // n_row
    for step, out in zip(steps, outs):
        owner = lax.rem(row + step, n_row)
        mine = total[pl.ds(owner * blocks_here, blocks_here)]
        out[...] = mine.reshape(out.shape).astype(BF16)


def copy_kernel(source, target, sem):
    copy = pltpu.make_async_copy(source, target, sem)
    copy.start()
    copy.wait()


def dense_kernel(parts, weight, cotangent, activated, grad_agg):
    total = parts[0].astype(F32)
    for chip in range(1, parts.shape[0]):
        total += parts[chip].astype(F32)
    aggregated = total.astype(BF16)
    pre = jnp.dot(aggregated, weight[...], preferred_element_type=F32)
    sigma = jax.nn.sigmoid(pre)
    activated[...] = (pre * sigma).astype(BF16)
    grad_pre = (cotangent[...].astype(F32) * sigma * (1.0 + pre * (1.0 - sigma))).astype(BF16)
    local_weight = lax.dot_general(
        aggregated, grad_pre, (((0,), (0,)), ((), ())), preferred_element_type=F32
    ).astype(BF16)
    grad = lax.dot_general(
        grad_pre, weight[...], (((1,), (1,)), ((), ())), preferred_element_type=F32
    ).astype(BF16)
    nodes = grad.shape[0]
    strip = grad_agg.shape[1] - nodes
    for chip in range(grad_agg.shape[0]):
        grad_agg[chip, :nodes] = grad
        grad_agg[chip, nodes:] = local_weight[chip * strip : (chip + 1) * strip]


def turn(size, step):
    return [(i, (i + step) % size) for i in range(size)]


def add_partners(value, size, distances):
    for other in [
        lax.ppermute(value, "row", [(i, i ^ distance) for i in range(size)])
        for distance in distances
    ]:
        value = value + other
    return value


def per_device(features, weight, cotangent, blk_vals, blk_rows, blk_cols, blk_count):
    n_row, n_col = lax.axis_size("row"), lax.axis_size("col")
    nodes, width = cotangent.shape
    slots, side = blk_vals.shape[2], blk_vals.shape[3]
    here = nodes // side
    chips = n_col // 2
    chunk = slots // 6
    place = jnp.stack([lax.axis_index("col") % 2, lax.axis_index("row")]).astype(jnp.int32)
    in_hbm = functools.partial(pltpu.with_memory_space_constraint, memory_space=pltpu.HBM)
    scalars = (place, blk_count[0], in_hbm(blk_rows[0, 0]), in_hbm(blk_cols[0, 0]))
    values = in_hbm(blk_vals[0, 0])
    smem = pl.BlockSpec(memory_space=pltpu.SMEM)
    vmem = pl.BlockSpec(memory_space=pltpu.VMEM)
    near = pl.BlockSpec(memory_space=pl.ANY)
    hbm = pl.BlockSpec(memory_space=pltpu.HBM)
    swap = [(i, i ^ 1) for i in range(n_col)]
    same_core = [list(range(core, n_col, 2)) for core in range(2)]
    work = 2 * slots * side * side * width

    own = pl.pallas_call(
        copy_kernel,
        out_shape=jax.ShapeDtypeStruct((here, side, width), BF16),
        in_specs=[hbm],
        out_specs=vmem,
        scratch_shapes=[pltpu.SemaphoreType.DMA],
        compiler_params=pltpu.CompilerParams(vmem_limit_bytes=4 * MIB),
    )(in_hbm(features.reshape(here, side, width)))
    steps = [0] + sorted(range(1, n_row), key=lambda k: (min(k, n_row - k), k))
    pieces = [own] + [lax.ppermute(own, "row", turn(n_row, k)) for k in steps[1:]]

    send, keep = pl.pallas_call(
        functools.partial(forward_kernel, chunk, steps),
        out_shape=(
            jax.ShapeDtypeStruct((chips, nodes, width), BF16),
            jax.ShapeDtypeStruct((chips, nodes, width), F32),
        ),
        in_specs=[smem] * 2 + [hbm] * 3 + [near] * n_row,
        out_specs=(vmem, vmem),
        scratch_shapes=[
            pltpu.SMEM((slots,), jnp.int32),
            pltpu.SMEM((slots,), jnp.int32),
            pltpu.VMEM((slots, side, side), BF16),
            pltpu.VMEM((here * n_row, side, width), BF16),
            pltpu.VMEM((here * n_col + 1, side, width), F32),
            pltpu.SemaphoreType.DMA((2,)),
            pltpu.SemaphoreType.DMA((slots // chunk,)),
            pltpu.SemaphoreType.DMA((n_row,)),
        ],
        compiler_params=pltpu.CompilerParams(vmem_limit_bytes=40 * MIB),
        cost_estimate=pl.CostEstimate(flops=work, bytes_accessed=14 * MIB, transcendentals=0),
    )(*scalars, values, *pieces)

    arrived = lax.ppermute(send, "col", swap)
    shares = (keep + arrived.astype(F32)).astype(BF16)
    parts = lax.all_to_all(shares, "col", 0, 0, tiled=True, axis_index_groups=same_core)

    strip = width // chips
    activated, grad_agg = pl.pallas_call(
        dense_kernel,
        out_shape=(
            jax.ShapeDtypeStruct((nodes, width), BF16),
            jax.ShapeDtypeStruct((chips, nodes + strip, width), BF16),
        ),
        in_specs=[vmem] * 3,
        out_specs=(vmem,) * 2,
        compiler_params=pltpu.CompilerParams(vmem_limit_bytes=24 * MIB),
        cost_estimate=pl.CostEstimate(
            flops=6 * nodes * width * width, bytes_accessed=5 * MIB, transcendentals=nodes * width
        ),
    )(parts, weight, cotangent)

    same = lax.all_to_all(grad_agg, "col", 0, 0, tiled=True, axis_index_groups=same_core)
    other = lax.ppermute(same, "col", swap)
    strips = jnp.sum(same[:, nodes:].astype(F32), axis=0)
    strips = add_partners(strips, n_row, [1])
    same, other, strips = lax.optimization_barrier((same, other, strips))
    strips = add_partners(strips, n_row, range(2, n_row, 2))

    shares = pl.pallas_call(
        functools.partial(backward_kernel, chunk, steps),
        out_shape=(jax.ShapeDtypeStruct((nodes, width), BF16),) * n_row,
        in_specs=[smem] * 2 + [hbm] * 3 + [near] * 2,
        out_specs=(vmem,) * n_row,
        scratch_shapes=[
            pltpu.SMEM((slots,), jnp.int32),
            pltpu.SMEM((slots,), jnp.int32),
            pltpu.VMEM((slots, side, side), BF16),
            pltpu.VMEM((2, chips, nodes + strip, width), BF16),
            pltpu.VMEM((here * n_row + 1, side, width), F32),
            pltpu.SemaphoreType.DMA((2,)),
            pltpu.SemaphoreType.DMA((slots // chunk,)),
            pltpu.SemaphoreType.DMA((2,)),
        ],
        compiler_params=pltpu.CompilerParams(vmem_limit_bytes=40 * MIB),
        cost_estimate=pl.CostEstimate(flops=work, bytes_accessed=11 * MIB, transcendentals=0),
    )(*scalars, values, same, other)

    shares, strips = lax.optimization_barrier((shares, strips))
    order = list(zip(steps, shares))[::-1]
    far, close, own_share = order[: n_row // 2], order[n_row // 2 : -1], shares[0]
    moved = [lax.ppermute(share, "row", turn(n_row, step)) for step, share in far]
    copies = jnp.broadcast_to(strips[None], (n_col, strip, width))
    every = lax.all_to_all(copies, "col", 0, 0, tiled=True)
    every, held = lax.optimization_barrier((every, [share for unused, share in close]))
    moved += [
        lax.ppermute(share, "row", turn(n_row, step)) for (step, unused), share in zip(close, held)
    ]
    total = own_share.astype(F32)
    for share in moved:
        total += share.astype(F32)
    grad_features = total.astype(BF16).reshape(1, nodes, width)
    grad_weight = jnp.sum(every.reshape(chips, 2, strip, width), axis=1).reshape(width, width)
    return (activated, grad_weight, grad_features)


def solution(mesh):
    return jax.shard_map(
        per_device,
        mesh=mesh,
        in_specs=(
            P("col", "row", None),
            P(),
            P(("row", "col"), None),
            P("row", "col", None, None, None),
            P("row", "col", None),
            P("row", "col", None),
            P("row", "col"),
        ),
        out_specs=(P(("row", "col"), None), P(), P("col", "row", None)),
        check_vma=False,
    )
```

```python
import functools

import jax
import jax.numpy as jnp
from jax import lax
from jax.experimental import pallas as pl
from jax.experimental.pallas import tpu as pltpu
from jax.sharding import PartitionSpec as P

BF16 = jnp.bfloat16
F32 = jnp.float32
UNROLL = 32
MIB = 1 << 20


def start_lists(sources, targets, sems):
    copies = [
        pltpu.make_async_copy(source, target, sems.at[at])
        for at, (source, target) in enumerate(zip(sources, targets))
    ]
    for copy in copies:
        copy.start()
    return copies


def start_chunks(live, vals_hbm, vals, sems, chunk):
    for piece in range(vals.shape[0] // chunk):

        @pl.when(piece * chunk < live)
        def _():
            part = pl.ds(piece * chunk, chunk)
            pltpu.make_async_copy(vals_hbm.at[part], vals.at[part], sems.at[piece]).start()


def each_live_slot(live, vals_hbm, vals, sems, chunk, one_slot):
    def one_chunk(piece, unused):
        part = pl.ds(piece * chunk, chunk)
        pltpu.make_async_copy(vals_hbm.at[part], vals.at[part], sems.at[piece]).wait()

        def one_group(group, unused):
            for lane in range(UNROLL):
                slot = piece * chunk + group * UNROLL + lane
                one_slot(slot, slot < live)
            return unused

        groups = (jnp.minimum(chunk, live - piece * chunk) + UNROLL - 1) // UNROLL
        return lax.fori_loop(0, groups, one_group, unused)

    lax.fori_loop(0, (live + chunk - 1) // chunk, one_chunk, 0)


def forward_kernel(chunk, steps, place, count, rows_hbm, cols_hbm, vals_hbm, *refs):
    n_row = len(refs) - 10
    pieces = refs[:n_row]
    send, keep, rows, cols, vals, panel, total, index_sems, val_sems, piece_sems = refs[n_row:]
    core, row, live = place[0], place[1], count[0]
    blocks_here = pieces[0].shape[0]
    copies = start_lists((rows_hbm, cols_hbm), (rows, cols), index_sems)
    for at, (step, piece) in enumerate(zip(steps, pieces)):
        owner = lax.rem(row + n_row - step, n_row)
        copies.append(
            pltpu.make_async_copy(
                piece, panel.at[pl.ds(owner * blocks_here, blocks_here)], piece_sems.at[at]
            )
        )
        copies[-1].start()
    start_chunks(live, vals_hbm, vals, val_sems, chunk)
    spare = total.shape[0] - 1

    def clear(block, unused):
        total[block] = jnp.zeros(total.shape[1:], F32)
        return unused

    lax.fori_loop(0, spare, clear, 0)
    for copy in copies:
        copy.wait()

    def one_slot(slot, alive):
        target = jnp.where(alive, rows[slot], spare)
        total[target] += jnp.dot(vals[slot], panel[cols[slot]], preferred_element_type=F32)

    each_live_slot(live, vals_hbm, vals, val_sems, chunk, one_slot)
    side, width = total.shape[1:]

    def split(chip, unused):
        first = 2 * blocks_here * chip
        other = total[pl.ds(first + blocks_here * (1 - core), blocks_here)]
        mine = total[pl.ds(first + blocks_here * core, blocks_here)]
        send[chip] = other.reshape(blocks_here * side, width).astype(BF16)
        keep[chip] = mine.reshape(blocks_here * side, width)
        return unused

    lax.fori_loop(0, send.shape[0], split, 0)


def backward_kernel(chunk, steps, place, count, rows_hbm, cols_hbm, vals_hbm, same, other, strip, *refs):
    n_row = len(steps)
    outs = refs[:n_row]
    rows, cols, vals, grads, total, index_sems, val_sems, grad_sems = refs[n_row:]
    core, row, live = place[0], place[1], count[0]
    side = total.shape[1]
    copies = [
        pltpu.make_async_copy(same, grads.at[core], grad_sems.at[0]),
        pltpu.make_async_copy(other, grads.at[1 - core], grad_sems.at[1]),
    ]
    for copy in copies:
        copy.start()
    copies += start_lists((rows_hbm, cols_hbm), (rows, cols), index_sems)
    start_chunks(live, vals_hbm, vals, val_sems, chunk)
    spare = total.shape[0] - 1
    for block in range(spare):
        total[block] = jnp.zeros(total.shape[1:], F32)
    for copy in copies:
        copy.wait()

    def one_slot(slot, alive):
        target = jnp.where(alive, cols[slot], spare)
        block = rows[slot]
        first = pl.multiple_of((block & 1) * side, side)
        picked = grads[(block >> 1) & 1, block >> 2, pl.ds(first, side)]
        total[target] += lax.dot_general(
            vals[slot], picked, (((0,), (0,)), ((), ())), preferred_element_type=F32
        )

    each_live_slot(live, vals_hbm, vals, val_sems, chunk, one_slot)
    blocks_here = spare // n_row
    nodes = blocks_here * side
    high = strip[...].astype(BF16)
    tail = jnp.concatenate([high, (strip[...] - high.astype(F32)).astype(BF16)], axis=0)
    for step, out in zip(steps, outs):
        owner = lax.rem(row + step, n_row)
        mine = total[pl.ds(owner * blocks_here, blocks_here)]
        out[:nodes] = mine.reshape(nodes, out.shape[1]).astype(BF16)
        out[nodes:] = tail


def copy_kernel(source, target, sem):
    copy = pltpu.make_async_copy(source, target, sem)
    copy.start()
    copy.wait()


def dense_kernel(n_row, place, parts, weight, cotangent, activated, grad_agg, *refs):
    strips, local_weight = refs[:n_row], refs[n_row]
    total = parts[0].astype(F32)
    for chip in range(1, parts.shape[0]):
        total += parts[chip].astype(F32)
    aggregated = total.astype(BF16)
    pre = jnp.dot(aggregated, weight[...], preferred_element_type=F32)
    sigma = jax.nn.sigmoid(pre)
    activated[...] = (pre * sigma).astype(BF16)
    grad_pre = (cotangent[...].astype(F32) * sigma * (1.0 + pre * (1.0 - sigma))).astype(BF16)
    grad = lax.dot_general(
        grad_pre, weight[...], (((1,), (1,)), ((), ())), preferred_element_type=F32
    ).astype(BF16)
    for chip in range(grad_agg.shape[0]):
        grad_agg[chip] = grad
    local_weight[...] = lax.dot_general(
        aggregated, grad_pre, (((0,), (0,)), ((), ())), preferred_element_type=F32
    )
    rows_strip = strips[0].shape[0]
    for step, strip in enumerate(strips):
        owner = lax.rem(place[1] + step, n_row)
        first = pl.multiple_of(owner * rows_strip, rows_strip)
        strip[...] = local_weight[pl.ds(first, rows_strip)]


def last_kernel(steps, place, *refs):
    n_row = len(steps)
    shares, (grad_features, grad_weight) = refs[:n_row], refs[n_row:]
    nodes = grad_features.shape[0]
    rows_strip = grad_weight.shape[0] // n_row
    total = shares[0][:nodes].astype(F32)
    for share in shares[1:]:
        total += share[:nodes].astype(F32)
    grad_features[...] = total.astype(BF16)
    for step, share in zip(steps, shares):
        owner = lax.rem(place[1] + n_row - step, n_row)
        first = pl.multiple_of(owner * rows_strip, rows_strip)
        high, low = share[nodes : nodes + rows_strip], share[nodes + rows_strip :]
        grad_weight[pl.ds(first, rows_strip)] = high.astype(F32) + low.astype(F32)


def turn(size, step):
    return [(i, (i + step) % size) for i in range(size)]


def add_partners(value, axis, size, distances):
    for other in [
        lax.ppermute(value, axis, [(i, i ^ distance) for i in range(size)])
        for distance in distances
    ]:
        value = value + other
    return value


def per_device(features, weight, cotangent, blk_vals, blk_rows, blk_cols, blk_count):
    n_row, n_col = lax.axis_size("row"), lax.axis_size("col")
    nodes, width = cotangent.shape
    slots, side = blk_vals.shape[2], blk_vals.shape[3]
    here = nodes // side
    chips = n_col // 2
    chunk = slots // 6
    place = jnp.stack([lax.axis_index("col") % 2, lax.axis_index("row")]).astype(jnp.int32)
    in_hbm = functools.partial(pltpu.with_memory_space_constraint, memory_space=pltpu.HBM)
    scalars = (place, blk_count[0], in_hbm(blk_rows[0, 0]), in_hbm(blk_cols[0, 0]))
    values = in_hbm(blk_vals[0, 0])
    smem = pl.BlockSpec(memory_space=pltpu.SMEM)
    vmem = pl.BlockSpec(memory_space=pltpu.VMEM)
    near = pl.BlockSpec(memory_space=pl.ANY)
    hbm = pl.BlockSpec(memory_space=pltpu.HBM)
    swap = [(i, i ^ 1) for i in range(n_col)]
    same_core = [list(range(core, n_col, 2)) for core in range(2)]
    work = 2 * slots * side * side * width

    own = pl.pallas_call(
        copy_kernel,
        out_shape=jax.ShapeDtypeStruct((here, side, width), BF16),
        in_specs=[hbm],
        out_specs=vmem,
        scratch_shapes=[pltpu.SemaphoreType.DMA],
        compiler_params=pltpu.CompilerParams(vmem_limit_bytes=4 * MIB),
    )(in_hbm(features.reshape(here, side, width)))
    steps = [0] + sorted(range(1, n_row), key=lambda k: (min(k, n_row - k), k))
    pieces = [own] + [lax.ppermute(own, "row", turn(n_row, k)) for k in steps[1:]]

    send, keep = pl.pallas_call(
        functools.partial(forward_kernel, chunk, steps),
        out_shape=(
            jax.ShapeDtypeStruct((chips, nodes, width), BF16),
            jax.ShapeDtypeStruct((chips, nodes, width), F32),
        ),
        in_specs=[smem] * 2 + [hbm] * 3 + [near] * n_row,
        out_specs=(vmem, vmem),
        scratch_shapes=[
            pltpu.SMEM((slots,), jnp.int32),
            pltpu.SMEM((slots,), jnp.int32),
            pltpu.VMEM((slots, side, side), BF16),
            pltpu.VMEM((here * n_row, side, width), BF16),
            pltpu.VMEM((here * n_col + 1, side, width), F32),
            pltpu.SemaphoreType.DMA((2,)),
            pltpu.SemaphoreType.DMA((slots // chunk,)),
            pltpu.SemaphoreType.DMA((n_row,)),
        ],
        compiler_params=pltpu.CompilerParams(vmem_limit_bytes=40 * MIB),
        cost_estimate=pl.CostEstimate(flops=work, bytes_accessed=14 * MIB, transcendentals=0),
    )(*scalars, values, *pieces)

    arrived = lax.ppermute(send, "col", swap)
    shares = (keep + arrived.astype(F32)).astype(BF16)
    parts = lax.all_to_all(shares, "col", 0, 0, tiled=True, axis_index_groups=same_core)

    rows_strip = width // n_row
    activated, grad_agg, *strips = pl.pallas_call(
        functools.partial(dense_kernel, n_row),
        out_shape=(
            jax.ShapeDtypeStruct((nodes, width), BF16),
            jax.ShapeDtypeStruct((chips, nodes, width), BF16),
        )
        + (jax.ShapeDtypeStruct((rows_strip, width), F32),) * n_row,
        in_specs=[smem] + [vmem] * 3,
        out_specs=(vmem,) * (2 + n_row),
        scratch_shapes=[pltpu.VMEM((width, width), F32)],
        compiler_params=pltpu.CompilerParams(vmem_limit_bytes=24 * MIB),
        cost_estimate=pl.CostEstimate(
            flops=6 * nodes * width * width, bytes_accessed=5 * MIB, transcendentals=nodes * width
        ),
    )(place, parts, weight, cotangent)

    same = lax.all_to_all(grad_agg, "col", 0, 0, tiled=True, axis_index_groups=same_core)
    moved = [lax.ppermute(strips[k], "row", turn(n_row, k)) for k in steps[:0:-1]]
    strip = strips[0]
    for other_strip in moved:
        strip = strip + other_strip
    strip = add_partners(strip, "col", n_col, [1])
    strip = add_partners(strip, "col", n_col, [2, 4, 6])
    strip = add_partners(strip, "col", n_col, [8, 16, 24])
    same, strip = lax.optimization_barrier((same, strip))
    other = lax.ppermute(same, "col", swap)

    shares = pl.pallas_call(
        functools.partial(backward_kernel, chunk, steps),
        out_shape=(jax.ShapeDtypeStruct((nodes + 2 * rows_strip, width), BF16),) * n_row,
        in_specs=[smem] * 2 + [hbm] * 3 + [near] * 2 + [vmem],
        out_specs=(vmem,) * n_row,
        scratch_shapes=[
            pltpu.SMEM((slots,), jnp.int32),
            pltpu.SMEM((slots,), jnp.int32),
            pltpu.VMEM((slots, side, side), BF16),
            pltpu.VMEM((2, chips, nodes, width), BF16),
            pltpu.VMEM((here * n_row + 1, side, width), F32),
            pltpu.SemaphoreType.DMA((2,)),
            pltpu.SemaphoreType.DMA((slots // chunk,)),
            pltpu.SemaphoreType.DMA((2,)),
        ],
        compiler_params=pltpu.CompilerParams(vmem_limit_bytes=40 * MIB),
        cost_estimate=pl.CostEstimate(flops=work, bytes_accessed=11 * MIB, transcendentals=0),
    )(*scalars, values, same, other, strip)

    shares = [shares[0]] + [
        lax.ppermute(share, "row", turn(n_row, step)) for step, share in zip(steps[1:], shares[1:])
    ]
    grad_features, grad_weight = pl.pallas_call(
        functools.partial(last_kernel, steps),
        out_shape=(
            jax.ShapeDtypeStruct((nodes, width), BF16),
            jax.ShapeDtypeStruct((width, width), F32),
        ),
        in_specs=[smem] + [vmem] * n_row,
        out_specs=(vmem, vmem),
        compiler_params=pltpu.CompilerParams(vmem_limit_bytes=16 * MIB),
    )(place, *shares)
    grad_features = grad_features.reshape(1, nodes, width)
    return (activated, grad_weight, grad_features)


def solution(mesh):
    return jax.shard_map(
        per_device,
        mesh=mesh,
        in_specs=(
            P("col", "row", None),
            P(),
            P(("row", "col"), None),
            P("row", "col", None, None, None),
            P("row", "col", None),
            P("row", "col", None),
            P("row", "col"),
        ),
        out_specs=(P(("row", "col"), None), P(), P("col", "row", None)),
        check_vma=False,
    )
```

```python
import functools

import jax
import jax.numpy as jnp
from jax import lax
from jax.experimental import pallas as pl
from jax.experimental.pallas import tpu as pltpu
from jax.sharding import PartitionSpec as P

BF16 = jnp.bfloat16
F32 = jnp.float32
UNROLL = 32
MIB = 1 << 20


def start_lists(sources, targets, sems):
    copies = [
        pltpu.make_async_copy(source, target, sems.at[at])
        for at, (source, target) in enumerate(zip(sources, targets))
    ]
    for copy in copies:
        copy.start()
    return copies


def start_chunks(live, vals_hbm, vals, sems, chunk):
    for piece in range(vals.shape[0] // chunk):

        @pl.when(piece * chunk < live)
        def _():
            part = pl.ds(piece * chunk, chunk)
            pltpu.make_async_copy(vals_hbm.at[part], vals.at[part], sems.at[piece]).start()


def each_live_slot(live, vals_hbm, vals, sems, chunk, one_slot):
    def one_chunk(piece, unused):
        part = pl.ds(piece * chunk, chunk)
        pltpu.make_async_copy(vals_hbm.at[part], vals.at[part], sems.at[piece]).wait()

        def one_group(group, unused):
            for lane in range(UNROLL):
                slot = piece * chunk + group * UNROLL + lane
                one_slot(slot, slot < live)
            return unused

        groups = (jnp.minimum(chunk, live - piece * chunk) + UNROLL - 1) // UNROLL
        return lax.fori_loop(0, groups, one_group, unused)

    lax.fori_loop(0, (live + chunk - 1) // chunk, one_chunk, 0)


def forward_kernel(chunk, steps, place, count, rows_hbm, cols_hbm, vals_hbm, *refs):
    n_row = len(refs) - 10
    pieces = refs[:n_row]
    send, keep, rows, cols, vals, panel, total, index_sems, val_sems, piece_sems = refs[n_row:]
    core, row, live = place[0], place[1], count[0]
    blocks_here = pieces[0].shape[0]
    copies = start_lists((rows_hbm, cols_hbm), (rows, cols), index_sems)
    for at, (step, piece) in enumerate(zip(steps, pieces)):
        owner = lax.rem(row + n_row - step, n_row)
        copies.append(
            pltpu.make_async_copy(
                piece, panel.at[pl.ds(owner * blocks_here, blocks_here)], piece_sems.at[at]
            )
        )
        copies[-1].start()
    start_chunks(live, vals_hbm, vals, val_sems, chunk)
    spare = total.shape[0] - 1

    def clear(block, unused):
        total[block] = jnp.zeros(total.shape[1:], F32)
        return unused

    lax.fori_loop(0, spare, clear, 0)
    for copy in copies:
        copy.wait()

    def one_slot(slot, alive):
        target = jnp.where(alive, rows[slot], spare)
        total[target] += jnp.dot(vals[slot], panel[cols[slot]], preferred_element_type=F32)

    each_live_slot(live, vals_hbm, vals, val_sems, chunk, one_slot)
    side, width = total.shape[1:]

    def split(chip, unused):
        first = 2 * blocks_here * chip
        other = total[pl.ds(first + blocks_here * (1 - core), blocks_here)]
        mine = total[pl.ds(first + blocks_here * core, blocks_here)]
        send[chip] = other.reshape(blocks_here * side, width).astype(BF16)
        keep[chip] = mine.reshape(blocks_here * side, width)
        return unused

    lax.fori_loop(0, send.shape[0], split, 0)


def backward_kernel(chunk, steps, place, count, rows_hbm, cols_hbm, vals_hbm, same, other, *refs):
    n_row = len(steps)
    outs = refs[:n_row]
    rows, cols, vals, grads, total, index_sems, val_sems, grad_sems = refs[n_row:]
    core, row, live = place[0], place[1], count[0]
    side = total.shape[1]
    copies = [
        pltpu.make_async_copy(same, grads.at[core], grad_sems.at[0]),
        pltpu.make_async_copy(other, grads.at[1 - core], grad_sems.at[1]),
    ]
    for copy in copies:
        copy.start()
    copies += start_lists((rows_hbm, cols_hbm), (rows, cols), index_sems)
    start_chunks(live, vals_hbm, vals, val_sems, chunk)
    spare = total.shape[0] - 1
    for block in range(spare):
        total[block] = jnp.zeros(total.shape[1:], F32)
    for copy in copies:
        copy.wait()

    def one_slot(slot, alive):
        target = jnp.where(alive, cols[slot], spare)
        block = rows[slot]
        first = pl.multiple_of((block & 1) * side, side)
        picked = grads[(block >> 1) & 1, block >> 2, pl.ds(first, side)]
        total[target] += lax.dot_general(
            vals[slot], picked, (((0,), (0,)), ((), ())), preferred_element_type=F32
        )

    each_live_slot(live, vals_hbm, vals, val_sems, chunk, one_slot)
    blocks_here = spare // n_row
    for step, out in zip(steps, outs):
        owner = lax.rem(row + step, n_row)
        mine = total[pl.ds(owner * blocks_here, blocks_here)]
        out[...] = mine.reshape(out.shape).astype(BF16)


def copy_kernel(source, target, sem):
    copy = pltpu.make_async_copy(source, target, sem)
    copy.start()
    copy.wait()


def dense_kernel(parts, weight, cotangent, activated, grad_agg, local_weight):
    total = parts[0].astype(F32)
    for chip in range(1, parts.shape[0]):
        total += parts[chip].astype(F32)
    aggregated = total.astype(BF16)
    pre = jnp.dot(aggregated, weight[...], preferred_element_type=F32)
    sigma = jax.nn.sigmoid(pre)
    activated[...] = (pre * sigma).astype(BF16)
    grad_pre = (cotangent[...].astype(F32) * sigma * (1.0 + pre * (1.0 - sigma))).astype(BF16)
    grad = lax.dot_general(
        grad_pre, weight[...], (((1,), (1,)), ((), ())), preferred_element_type=F32
    ).astype(BF16)
    for chip in range(grad_agg.shape[0]):
        grad_agg[chip] = grad
    local_weight[...] = lax.dot_general(
        aggregated, grad_pre, (((0,), (0,)), ((), ())), preferred_element_type=F32
    )


def turn(size, step):
    return [(i, (i + step) % size) for i in range(size)]


def add_partners(value, axis, size, distances):
    for other in [
        lax.ppermute(value, axis, [(i, i ^ distance) for i in range(size)])
        for distance in distances
    ]:
        value = value + other
    return value


def sum_halves(value, axis, size, index):
    distance = size // 2
    while distance:
        half = value.shape[0] // 2
        upper = (index // distance) % 2 == 1
        sent = jnp.where(upper, value[:half], value[half:])
        kept = jnp.where(upper, value[half:], value[:half])
        value = kept + lax.ppermute(sent, axis, [(i, i ^ distance) for i in range(size)])
        distance //= 2
    return value


def per_device(features, weight, cotangent, blk_vals, blk_rows, blk_cols, blk_count):
    n_row, n_col = lax.axis_size("row"), lax.axis_size("col")
    nodes, width = cotangent.shape
    slots, side = blk_vals.shape[2], blk_vals.shape[3]
    here = nodes // side
    chips = n_col // 2
    chunk = slots // 6
    place = jnp.stack([lax.axis_index("col") % 2, lax.axis_index("row")]).astype(jnp.int32)
    in_hbm = functools.partial(pltpu.with_memory_space_constraint, memory_space=pltpu.HBM)
    scalars = (place, blk_count[0], in_hbm(blk_rows[0, 0]), in_hbm(blk_cols[0, 0]))
    values = in_hbm(blk_vals[0, 0])
    smem = pl.BlockSpec(memory_space=pltpu.SMEM)
    vmem = pl.BlockSpec(memory_space=pltpu.VMEM)
    near = pl.BlockSpec(memory_space=pl.ANY)
    hbm = pl.BlockSpec(memory_space=pltpu.HBM)
    swap = [(i, i ^ 1) for i in range(n_col)]
    same_core = [list(range(core, n_col, 2)) for core in range(2)]
    work = 2 * slots * side * side * width

    own = pl.pallas_call(
        copy_kernel,
        out_shape=jax.ShapeDtypeStruct((here, side, width), BF16),
        in_specs=[hbm],
        out_specs=vmem,
        scratch_shapes=[pltpu.SemaphoreType.DMA],
        compiler_params=pltpu.CompilerParams(vmem_limit_bytes=4 * MIB),
    )(in_hbm(features.reshape(here, side, width)))
    steps = [0] + sorted(range(1, n_row), key=lambda k: (min(k, n_row - k), k))
    pieces = [own] + [lax.ppermute(own, "row", turn(n_row, k)) for k in steps[1:]]

    send, keep = pl.pallas_call(
        functools.partial(forward_kernel, chunk, steps),
        out_shape=(
            jax.ShapeDtypeStruct((chips, nodes, width), BF16),
            jax.ShapeDtypeStruct((chips, nodes, width), F32),
        ),
        in_specs=[smem] * 2 + [hbm] * 3 + [near] * n_row,
        out_specs=(vmem, vmem),
        scratch_shapes=[
            pltpu.SMEM((slots,), jnp.int32),
            pltpu.SMEM((slots,), jnp.int32),
            pltpu.VMEM((slots, side, side), BF16),
            pltpu.VMEM((here * n_row, side, width), BF16),
            pltpu.VMEM((here * n_col + 1, side, width), F32),
            pltpu.SemaphoreType.DMA((2,)),
            pltpu.SemaphoreType.DMA((slots // chunk,)),
            pltpu.SemaphoreType.DMA((n_row,)),
        ],
        compiler_params=pltpu.CompilerParams(vmem_limit_bytes=40 * MIB),
        cost_estimate=pl.CostEstimate(flops=work, bytes_accessed=14 * MIB, transcendentals=0),
    )(*scalars, values, *pieces)

    arrived = lax.ppermute(send, "col", swap)
    shares = (keep + arrived.astype(F32)).astype(BF16)
    parts = lax.all_to_all(shares, "col", 0, 0, tiled=True, axis_index_groups=same_core)

    rows_strip = width // n_row
    activated, grad_agg, local_weight = pl.pallas_call(
        dense_kernel,
        out_shape=(
            jax.ShapeDtypeStruct((nodes, width), BF16),
            jax.ShapeDtypeStruct((chips, nodes, width), BF16),
            jax.ShapeDtypeStruct((width, width), F32),
        ),
        in_specs=[vmem] * 3,
        out_specs=(vmem,) * 3,
        compiler_params=pltpu.CompilerParams(vmem_limit_bytes=24 * MIB),
        cost_estimate=pl.CostEstimate(
            flops=6 * nodes * width * width, bytes_accessed=5 * MIB, transcendentals=nodes * width
        ),
    )(parts, weight, cotangent)

    same = lax.all_to_all(grad_agg, "col", 0, 0, tiled=True, axis_index_groups=same_core)
    strip = sum_halves(local_weight, "row", n_row, lax.axis_index("row"))
    strip = add_partners(strip, "col", n_col, [1])
    strip = add_partners(strip, "col", n_col, [2, 4, 6])
    strip = add_partners(strip, "col", n_col, [8, 16, 24])
    same, strip = lax.optimization_barrier((same, strip))
    other = lax.ppermute(same, "col", swap)
    copies = jnp.broadcast_to(strip[None], (n_row, rows_strip, width))
    every = lax.all_to_all(copies, "row", 0, 0, tiled=True)
    grad_weight = every.reshape(width, width)

    shares = pl.pallas_call(
        functools.partial(backward_kernel, chunk, steps),
        out_shape=(jax.ShapeDtypeStruct((nodes, width), BF16),) * n_row,
        in_specs=[smem] * 2 + [hbm] * 3 + [near] * 2,
        out_specs=(vmem,) * n_row,
        scratch_shapes=[
            pltpu.SMEM((slots,), jnp.int32),
            pltpu.SMEM((slots,), jnp.int32),
            pltpu.VMEM((slots, side, side), BF16),
            pltpu.VMEM((2, chips, nodes, width), BF16),
            pltpu.VMEM((here * n_row + 1, side, width), F32),
            pltpu.SemaphoreType.DMA((2,)),
            pltpu.SemaphoreType.DMA((slots // chunk,)),
            pltpu.SemaphoreType.DMA((2,)),
        ],
        compiler_params=pltpu.CompilerParams(vmem_limit_bytes=40 * MIB),
        cost_estimate=pl.CostEstimate(flops=work, bytes_accessed=11 * MIB, transcendentals=0),
    )(*scalars, values, same, other)

    *shares, grad_weight = lax.optimization_barrier((*shares, grad_weight))
    total = shares[0].astype(F32)
    for step, share in list(zip(steps, shares))[:0:-1]:
        total += lax.ppermute(share, "row", turn(n_row, step)).astype(F32)
    grad_features = total.astype(BF16).reshape(1, nodes, width)
    return (activated, grad_weight, grad_features)


def solution(mesh):
    return jax.shard_map(
        per_device,
        mesh=mesh,
        in_specs=(
            P("col", "row", None),
            P(),
            P(("row", "col"), None),
            P("row", "col", None, None, None),
            P("row", "col", None),
            P("row", "col", None),
            P("row", "col"),
        ),
        out_specs=(P(("row", "col"), None), P(), P("col", "row", None)),
        check_vma=False,
    )
```

```python
import functools

import jax
import jax.numpy as jnp
from jax import lax
from jax.experimental import pallas as pl
from jax.experimental.pallas import tpu as pltpu
from jax.sharding import PartitionSpec as P

BF16 = jnp.bfloat16
F32 = jnp.float32
UNROLL = 32
MIB = 1 << 20


def start_lists(sources, targets, sems):
    copies = [
        pltpu.make_async_copy(source, target, sems.at[at])
        for at, (source, target) in enumerate(zip(sources, targets))
    ]
    for copy in copies:
        copy.start()
    return copies


def start_chunks(live, vals_hbm, vals, sems, chunk):
    for piece in range(vals.shape[0] // chunk):

        @pl.when(piece * chunk < live)
        def _():
            part = pl.ds(piece * chunk, chunk)
            pltpu.make_async_copy(vals_hbm.at[part], vals.at[part], sems.at[piece]).start()


def each_live_slot(live, vals_hbm, vals, sems, chunk, one_slot):
    def one_chunk(piece, unused):
        part = pl.ds(piece * chunk, chunk)
        pltpu.make_async_copy(vals_hbm.at[part], vals.at[part], sems.at[piece]).wait()

        def one_group(group, unused):
            for lane in range(UNROLL):
                slot = piece * chunk + group * UNROLL + lane
                one_slot(slot, slot < live)
            return unused

        groups = (jnp.minimum(chunk, live - piece * chunk) + UNROLL - 1) // UNROLL
        return lax.fori_loop(0, groups, one_group, unused)

    lax.fori_loop(0, (live + chunk - 1) // chunk, one_chunk, 0)


def forward_kernel(chunk, steps, place, count, rows_hbm, cols_hbm, vals_hbm, *refs):
    n_row = len(refs) - 10
    pieces = refs[:n_row]
    send, keep, rows, cols, vals, panel, total, index_sems, val_sems, piece_sems = refs[n_row:]
    core, row, live = place[0], place[1], count[0]
    blocks_here = pieces[0].shape[0]
    copies = start_lists((rows_hbm, cols_hbm), (rows, cols), index_sems)
    for at, (step, piece) in enumerate(zip(steps, pieces)):
        owner = lax.rem(row + n_row - step, n_row)
        copies.append(
            pltpu.make_async_copy(
                piece, panel.at[pl.ds(owner * blocks_here, blocks_here)], piece_sems.at[at]
            )
        )
        copies[-1].start()
    start_chunks(live, vals_hbm, vals, val_sems, chunk)
    spare = total.shape[0] - 1

    def clear(block, unused):
        total[block] = jnp.zeros(total.shape[1:], F32)
        return unused

    lax.fori_loop(0, spare, clear, 0)
    for copy in copies:
        copy.wait()

    def one_slot(slot, alive):
        target = jnp.where(alive, rows[slot], spare)
        total[target] += jnp.dot(vals[slot], panel[cols[slot]], preferred_element_type=F32)

    each_live_slot(live, vals_hbm, vals, val_sems, chunk, one_slot)
    side, width = total.shape[1:]

    def split(chip, unused):
        first = 2 * blocks_here * chip
        other = total[pl.ds(first + blocks_here * (1 - core), blocks_here)]
        mine = total[pl.ds(first + blocks_here * core, blocks_here)]
        send[chip] = other.reshape(blocks_here * side, width).astype(BF16)
        keep[chip] = mine.reshape(blocks_here * side, width)
        return unused

    lax.fori_loop(0, send.shape[0], split, 0)


def backward_kernel(chunk, steps, place, count, rows_hbm, cols_hbm, vals_hbm, same, other, *refs):
    n_row = len(steps)
    outs = refs[:n_row]
    rows, cols, vals, grads, total, index_sems, val_sems, grad_sems = refs[n_row:]
    core, row, live = place[0], place[1], count[0]
    side = total.shape[1]
    copies = [
        pltpu.make_async_copy(same, grads.at[core], grad_sems.at[0]),
        pltpu.make_async_copy(other, grads.at[1 - core], grad_sems.at[1]),
    ]
    for copy in copies:
        copy.start()
    copies += start_lists((rows_hbm, cols_hbm), (rows, cols), index_sems)
    start_chunks(live, vals_hbm, vals, val_sems, chunk)
    spare = total.shape[0] - 1
    for block in range(spare):
        total[block] = jnp.zeros(total.shape[1:], F32)
    for copy in copies:
        copy.wait()

    def one_slot(slot, alive):
        target = jnp.where(alive, cols[slot], spare)
        block = rows[slot]
        first = pl.multiple_of((block & 1) * side, side)
        picked = grads[(block >> 1) & 1, block >> 2, pl.ds(first, side)]
        total[target] += lax.dot_general(
            vals[slot], picked, (((0,), (0,)), ((), ())), preferred_element_type=F32
        )

    each_live_slot(live, vals_hbm, vals, val_sems, chunk, one_slot)
    blocks_here = spare // n_row
    for step, out in zip(steps, outs):
        owner = lax.rem(row + step, n_row)
        mine = total[pl.ds(owner * blocks_here, blocks_here)]
        out[...] = mine.reshape(out.shape).astype(BF16)


def dense_kernel(parts, weight, cotangent, activated, grad_agg):
    total = parts[0].astype(F32)
    for chip in range(1, parts.shape[0]):
        total += parts[chip].astype(F32)
    aggregated = total.astype(BF16)
    pre = jnp.dot(aggregated, weight[...], preferred_element_type=F32)
    sigma = jax.nn.sigmoid(pre)
    activated[...] = (pre * sigma).astype(BF16)
    grad_pre = (cotangent[...].astype(F32) * sigma * (1.0 + pre * (1.0 - sigma))).astype(BF16)
    local_weight = lax.dot_general(
        aggregated, grad_pre, (((0,), (0,)), ((), ())), preferred_element_type=F32
    ).astype(BF16)
    grad = lax.dot_general(
        grad_pre, weight[...], (((1,), (1,)), ((), ())), preferred_element_type=F32
    ).astype(BF16)
    nodes = grad.shape[0]
    strip = grad_agg.shape[1] - nodes
    for chip in range(grad_agg.shape[0]):
        grad_agg[chip, :nodes] = grad
        grad_agg[chip, nodes:] = local_weight[chip * strip : (chip + 1) * strip]


def turn(size, step):
    return [(i, (i + step) % size) for i in range(size)]


def add_partners(value, size, distances):
    for other in [
        lax.ppermute(value, "row", [(i, i ^ distance) for i in range(size)])
        for distance in distances
    ]:
        value = value + other
    return value


def per_device(features, weight, cotangent, blk_vals, blk_rows, blk_cols, blk_count):
    n_row, n_col = lax.axis_size("row"), lax.axis_size("col")
    nodes, width = cotangent.shape
    slots, side = blk_vals.shape[2], blk_vals.shape[3]
    here = nodes // side
    chips = n_col // 2
    chunk = slots // 6
    place = jnp.stack([lax.axis_index("col") % 2, lax.axis_index("row")]).astype(jnp.int32)
    in_hbm = functools.partial(pltpu.with_memory_space_constraint, memory_space=pltpu.HBM)
    scalars = (place, blk_count[0], in_hbm(blk_rows[0, 0]), in_hbm(blk_cols[0, 0]))
    values = in_hbm(blk_vals[0, 0])
    smem = pl.BlockSpec(memory_space=pltpu.SMEM)
    vmem = pl.BlockSpec(memory_space=pltpu.VMEM)
    near = pl.BlockSpec(memory_space=pl.ANY)
    hbm = pl.BlockSpec(memory_space=pltpu.HBM)
    swap = [(i, i ^ 1) for i in range(n_col)]
    same_core = [list(range(core, n_col, 2)) for core in range(2)]
    work = 2 * slots * side * side * width

    own = features.reshape(here, side, width)
    steps = [0] + sorted(range(1, n_row), key=lambda k: (min(k, n_row - k), k))
    arrival = [0] + steps[:0:-1]
    pieces = [in_hbm(own)] + [lax.ppermute(own, "row", turn(n_row, k)) for k in arrival[1:]]

    send, keep = pl.pallas_call(
        functools.partial(forward_kernel, chunk, arrival),
        out_shape=(
            jax.ShapeDtypeStruct((chips, nodes, width), BF16),
            jax.ShapeDtypeStruct((chips, nodes, width), F32),
        ),
        in_specs=[smem] * 2 + [hbm] * 4 + [near] * (n_row - 1),
        out_specs=(vmem, vmem),
        scratch_shapes=[
            pltpu.SMEM((slots,), jnp.int32),
            pltpu.SMEM((slots,), jnp.int32),
            pltpu.VMEM((slots, side, side), BF16),
            pltpu.VMEM((here * n_row, side, width), BF16),
            pltpu.VMEM((here * n_col + 1, side, width), F32),
            pltpu.SemaphoreType.DMA((2,)),
            pltpu.SemaphoreType.DMA((slots // chunk,)),
            pltpu.SemaphoreType.DMA((n_row,)),
        ],
        compiler_params=pltpu.CompilerParams(vmem_limit_bytes=40 * MIB),
        cost_estimate=pl.CostEstimate(flops=work, bytes_accessed=14 * MIB, transcendentals=0),
    )(*scalars, values, *pieces)

    arrived = lax.ppermute(send, "col", swap)
    shares = (keep + arrived.astype(F32)).astype(BF16)
    parts = lax.all_to_all(shares, "col", 0, 0, tiled=True, axis_index_groups=same_core)

    strip = width // chips
    activated, grad_agg = pl.pallas_call(
        dense_kernel,
        out_shape=(
            jax.ShapeDtypeStruct((nodes, width), BF16),
            jax.ShapeDtypeStruct((chips, nodes + strip, width), BF16),
        ),
        in_specs=[vmem] * 3,
        out_specs=(vmem,) * 2,
        compiler_params=pltpu.CompilerParams(vmem_limit_bytes=24 * MIB),
        cost_estimate=pl.CostEstimate(
            flops=6 * nodes * width * width, bytes_accessed=5 * MIB, transcendentals=nodes * width
        ),
    )(parts, weight, cotangent)

    same = lax.all_to_all(grad_agg, "col", 0, 0, tiled=True, axis_index_groups=same_core)
    other = lax.ppermute(same, "col", swap)
    strips = jnp.sum(same[:, nodes:].astype(F32), axis=0)
    strips = add_partners(strips, n_row, range(1, n_row // 2))
    same, other, strips = lax.optimization_barrier((same, other, strips))
    strips = add_partners(strips, n_row, [n_row // 2])

    shares = pl.pallas_call(
        functools.partial(backward_kernel, chunk, steps),
        out_shape=(jax.ShapeDtypeStruct((nodes, width), BF16),) * n_row,
        in_specs=[smem] * 2 + [hbm] * 3 + [near] * 2,
        out_specs=(vmem,) * n_row,
        scratch_shapes=[
            pltpu.SMEM((slots,), jnp.int32),
            pltpu.SMEM((slots,), jnp.int32),
            pltpu.VMEM((slots, side, side), BF16),
            pltpu.VMEM((2, chips, nodes + strip, width), BF16),
            pltpu.VMEM((here * n_row + 1, side, width), F32),
            pltpu.SemaphoreType.DMA((2,)),
            pltpu.SemaphoreType.DMA((slots // chunk,)),
            pltpu.SemaphoreType.DMA((2,)),
        ],
        compiler_params=pltpu.CompilerParams(vmem_limit_bytes=40 * MIB),
        cost_estimate=pl.CostEstimate(flops=work, bytes_accessed=11 * MIB, transcendentals=0),
    )(*scalars, values, same, other)

    shares, strips = lax.optimization_barrier((shares, strips))
    order = list(zip(steps, shares))[::-1]
    far, close, own_share = order[: n_row // 2], order[n_row // 2 : -1], shares[0]
    moved = [lax.ppermute(share, "row", turn(n_row, step)) for step, share in far]
    copies = jnp.broadcast_to(strips[None], (n_col, strip, width))
    every = lax.all_to_all(copies, "col", 0, 0, tiled=True)
    every, held = lax.optimization_barrier((every, [share for unused, share in close]))
    moved += [
        lax.ppermute(share, "row", turn(n_row, step)) for (step, unused), share in zip(close, held)
    ]
    total = own_share.astype(F32)
    for share in moved:
        total += share.astype(F32)
    grad_features = total.astype(BF16).reshape(1, nodes, width)
    grad_weight = jnp.sum(every.reshape(chips, 2, strip, width), axis=1).reshape(width, width)
    return (activated, grad_weight, grad_features)


def solution(mesh):
    return jax.shard_map(
        per_device,
        mesh=mesh,
        in_specs=(
            P("col", "row", None),
            P(),
            P(("row", "col"), None),
            P("row", "col", None, None, None),
            P("row", "col", None),
            P("row", "col", None),
            P("row", "col"),
        ),
        out_specs=(P(("row", "col"), None), P(), P("col", "row", None)),
        check_vma=False,
    )
```

```python
import functools

import jax
import jax.numpy as jnp
from jax import lax
from jax.experimental import pallas as pl
from jax.experimental.pallas import tpu as pltpu
from jax.sharding import PartitionSpec as P

BF16 = jnp.bfloat16
F32 = jnp.float32
UNROLL = 32
MIB = 1 << 20


def start_lists(sources, targets, sems):
    copies = [
        pltpu.make_async_copy(source, target, sems.at[at])
        for at, (source, target) in enumerate(zip(sources, targets))
    ]
    for copy in copies:
        copy.start()
    return copies


def start_chunks(live, vals_hbm, vals, sems, chunk):
    for piece in range(vals.shape[0] // chunk):

        @pl.when(piece * chunk < live)
        def _():
            part = pl.ds(piece * chunk, chunk)
            pltpu.make_async_copy(vals_hbm.at[part], vals.at[part], sems.at[piece]).start()


def each_live_slot(live, vals_hbm, vals, sems, chunk, one_slot):
    def one_chunk(piece, unused):
        part = pl.ds(piece * chunk, chunk)
        pltpu.make_async_copy(vals_hbm.at[part], vals.at[part], sems.at[piece]).wait()

        def one_group(group, unused):
            for lane in range(UNROLL):
                slot = piece * chunk + group * UNROLL + lane
                one_slot(slot, slot < live)
            return unused

        groups = (jnp.minimum(chunk, live - piece * chunk) + UNROLL - 1) // UNROLL
        return lax.fori_loop(0, groups, one_group, unused)

    lax.fori_loop(0, (live + chunk - 1) // chunk, one_chunk, 0)


def forward_kernel(chunk, steps, place, count, rows_hbm, cols_hbm, vals_hbm, *refs):
    n_row = len(refs) - 10
    pieces = refs[:n_row]
    send, keep, rows, cols, vals, panel, total, index_sems, val_sems, piece_sems = refs[n_row:]
    core, row, live = place[0], place[1], count[0]
    blocks_here = pieces[0].shape[0]
    copies = start_lists((rows_hbm, cols_hbm), (rows, cols), index_sems)
    for at, (step, piece) in enumerate(zip(steps, pieces)):
        owner = lax.rem(row + n_row - step, n_row)
        copies.append(
            pltpu.make_async_copy(
                piece, panel.at[pl.ds(owner * blocks_here, blocks_here)], piece_sems.at[at]
            )
        )
        copies[-1].start()
    start_chunks(live, vals_hbm, vals, val_sems, chunk)
    spare = total.shape[0] - 1

    def clear(block, unused):
        total[block] = jnp.zeros(total.shape[1:], F32)
        return unused

    lax.fori_loop(0, spare, clear, 0)
    for copy in copies:
        copy.wait()

    def one_slot(slot, alive):
        target = jnp.where(alive, rows[slot], spare)
        total[target] += jnp.dot(vals[slot], panel[cols[slot]], preferred_element_type=F32)

    each_live_slot(live, vals_hbm, vals, val_sems, chunk, one_slot)
    side, width = total.shape[1:]

    def split(chip, unused):
        first = 2 * blocks_here * chip
        other = total[pl.ds(first + blocks_here * (1 - core), blocks_here)]
        mine = total[pl.ds(first + blocks_here * core, blocks_here)]
        send[chip] = other.reshape(blocks_here * side, width).astype(BF16)
        keep[chip] = mine.reshape(blocks_here * side, width)
        return unused

    lax.fori_loop(0, send.shape[0], split, 0)


def backward_kernel(chunk, steps, place, count, rows_hbm, cols_hbm, vals_hbm, same, other, *refs):
    n_row = len(steps)
    outs = refs[:n_row]
    rows, cols, vals, grads, total, index_sems, val_sems, grad_sems = refs[n_row:]
    core, row, live = place[0], place[1], count[0]
    side = total.shape[1]
    copies = [
        pltpu.make_async_copy(same, grads.at[core], grad_sems.at[0]),
        pltpu.make_async_copy(other, grads.at[1 - core], grad_sems.at[1]),
    ]
    for copy in copies:
        copy.start()
    copies += start_lists((rows_hbm, cols_hbm), (rows, cols), index_sems)
    start_chunks(live, vals_hbm, vals, val_sems, chunk)
    spare = total.shape[0] - 1
    for block in range(spare):
        total[block] = jnp.zeros(total.shape[1:], F32)
    for copy in copies:
        copy.wait()

    def one_slot(slot, alive):
        target = jnp.where(alive, cols[slot], spare)
        block = rows[slot]
        first = pl.multiple_of((block & 1) * side, side)
        picked = grads[(block >> 1) & 1, block >> 2, pl.ds(first, side)]
        total[target] += lax.dot_general(
            vals[slot], picked, (((0,), (0,)), ((), ())), preferred_element_type=F32
        )

    each_live_slot(live, vals_hbm, vals, val_sems, chunk, one_slot)
    blocks_here = spare // n_row
    for step, out in zip(steps, outs):
        owner = lax.rem(row + step, n_row)
        mine = total[pl.ds(owner * blocks_here, blocks_here)]
        out[...] = mine.reshape(out.shape).astype(BF16)


def dense_kernel(parts, weight, cotangent, activated, grad_agg):
    total = parts[0].astype(F32)
    for chip in range(1, parts.shape[0]):
        total += parts[chip].astype(F32)
    aggregated = total.astype(BF16)
    pre = jnp.dot(aggregated, weight[...], preferred_element_type=F32)
    sigma = jax.nn.sigmoid(pre)
    activated[...] = (pre * sigma).astype(BF16)
    grad_pre = (cotangent[...].astype(F32) * sigma * (1.0 + pre * (1.0 - sigma))).astype(BF16)
    local_weight = lax.dot_general(
        aggregated, grad_pre, (((0,), (0,)), ((), ())), preferred_element_type=F32
    ).astype(BF16)
    grad = lax.dot_general(
        grad_pre, weight[...], (((1,), (1,)), ((), ())), preferred_element_type=F32
    ).astype(BF16)
    nodes = grad.shape[0]
    strip = grad_agg.shape[1] - nodes
    for chip in range(grad_agg.shape[0]):
        grad_agg[chip, :nodes] = grad
        grad_agg[chip, nodes:] = local_weight[chip * strip : (chip + 1) * strip]


def turn(size, step):
    return [(i, (i + step) % size) for i in range(size)]


def add_partners(value, size, distances):
    for other in [
        lax.ppermute(value, "row", [(i, i ^ distance) for i in range(size)])
        for distance in distances
    ]:
        value = value + other
    return value


def per_device(features, weight, cotangent, blk_vals, blk_rows, blk_cols, blk_count):
    n_row, n_col = lax.axis_size("row"), lax.axis_size("col")
    nodes, width = cotangent.shape
    slots, side = blk_vals.shape[2], blk_vals.shape[3]
    here = nodes // side
    chips = n_col // 2
    chunk = slots // 6
    place = jnp.stack([lax.axis_index("col") % 2, lax.axis_index("row")]).astype(jnp.int32)
    in_hbm = functools.partial(pltpu.with_memory_space_constraint, memory_space=pltpu.HBM)
    scalars = (place, blk_count[0], in_hbm(blk_rows[0, 0]), in_hbm(blk_cols[0, 0]))
    values = in_hbm(blk_vals[0, 0])
    smem = pl.BlockSpec(memory_space=pltpu.SMEM)
    vmem = pl.BlockSpec(memory_space=pltpu.VMEM)
    near = pl.BlockSpec(memory_space=pl.ANY)
    hbm = pl.BlockSpec(memory_space=pltpu.HBM)
    swap = [(i, i ^ 1) for i in range(n_col)]
    same_core = [list(range(core, n_col, 2)) for core in range(2)]
    work = 2 * slots * side * side * width

    own = features.reshape(here, side, width)
    steps = [0] + sorted(range(1, n_row), key=lambda k: (min(k, n_row - k), k))
    arrival = [0] + steps[:0:-1]
    pieces = [in_hbm(own)] + [lax.ppermute(own, "row", turn(n_row, k)) for k in arrival[1:]]

    send, keep = pl.pallas_call(
        functools.partial(forward_kernel, chunk, arrival),
        out_shape=(
            jax.ShapeDtypeStruct((chips, nodes, width), BF16),
            jax.ShapeDtypeStruct((chips, nodes, width), F32),
        ),
        in_specs=[smem] * 2 + [hbm] * 4 + [near] * (n_row - 1),
        out_specs=(vmem, vmem),
        scratch_shapes=[
            pltpu.SMEM((slots,), jnp.int32),
            pltpu.SMEM((slots,), jnp.int32),
            pltpu.VMEM((slots, side, side), BF16),
            pltpu.VMEM((here * n_row, side, width), BF16),
            pltpu.VMEM((here * n_col + 1, side, width), F32),
            pltpu.SemaphoreType.DMA((2,)),
            pltpu.SemaphoreType.DMA((slots // chunk,)),
            pltpu.SemaphoreType.DMA((n_row,)),
        ],
        compiler_params=pltpu.CompilerParams(vmem_limit_bytes=40 * MIB),
        cost_estimate=pl.CostEstimate(flops=work, bytes_accessed=14 * MIB, transcendentals=0),
    )(*scalars, values, *pieces)

    arrived = lax.ppermute(send, "col", swap)
    shares = (keep + arrived.astype(F32)).astype(BF16)
    parts = lax.all_to_all(shares, "col", 0, 0, tiled=True, axis_index_groups=same_core)

    strip = width // chips
    activated, grad_agg = pl.pallas_call(
        dense_kernel,
        out_shape=(
            jax.ShapeDtypeStruct((nodes, width), BF16),
            jax.ShapeDtypeStruct((chips, nodes + strip, width), BF16),
        ),
        in_specs=[vmem] * 3,
        out_specs=(vmem,) * 2,
        compiler_params=pltpu.CompilerParams(vmem_limit_bytes=24 * MIB),
        cost_estimate=pl.CostEstimate(
            flops=6 * nodes * width * width, bytes_accessed=5 * MIB, transcendentals=nodes * width
        ),
    )(parts, weight, cotangent)

    same = lax.all_to_all(grad_agg, "col", 0, 0, tiled=True, axis_index_groups=same_core)
    other = lax.ppermute(same, "col", swap)
    strips = jnp.sum(same[:, nodes:].astype(F32), axis=0)
    strips = add_partners(strips, n_row, [1])
    same, other, strips = lax.optimization_barrier((same, other, strips))
    strips = add_partners(strips, n_row, range(2, n_row, 2))

    shares = pl.pallas_call(
        functools.partial(backward_kernel, chunk, steps),
        out_shape=(jax.ShapeDtypeStruct((nodes, width), BF16),) * n_row,
        in_specs=[smem] * 2 + [hbm] * 3 + [near] * 2,
        out_specs=(vmem,) * n_row,
        scratch_shapes=[
            pltpu.SMEM((slots,), jnp.int32),
            pltpu.SMEM((slots,), jnp.int32),
            pltpu.VMEM((slots, side, side), BF16),
            pltpu.VMEM((2, chips, nodes + strip, width), BF16),
            pltpu.VMEM((here * n_row + 1, side, width), F32),
            pltpu.SemaphoreType.DMA((2,)),
            pltpu.SemaphoreType.DMA((slots // chunk,)),
            pltpu.SemaphoreType.DMA((2,)),
        ],
        compiler_params=pltpu.CompilerParams(vmem_limit_bytes=40 * MIB),
        cost_estimate=pl.CostEstimate(flops=work, bytes_accessed=11 * MIB, transcendentals=0),
    )(*scalars, values, same, other)

    shares, strips = lax.optimization_barrier((shares, strips))
    order = list(zip(steps, shares))[::-1]
    far, close, own_share = order[: n_row // 2], order[n_row // 2 : -1], shares[0]
    moved = [lax.ppermute(share, "row", turn(n_row, step)) for step, share in far]
    copies = jnp.broadcast_to(strips[None], (n_col, strip, width))
    every = lax.all_to_all(copies, "col", 0, 0, tiled=True)
    every, held = lax.optimization_barrier((every, [share for unused, share in close]))
    moved += [
        lax.ppermute(share, "row", turn(n_row, step)) for (step, unused), share in zip(close, held)
    ]
    total = own_share.astype(F32)
    for share in moved:
        total += share.astype(F32)
    grad_features = total.astype(BF16).reshape(1, nodes, width)
    grad_weight = jnp.sum(every.reshape(chips, 2, strip, width), axis=1).reshape(width, width)
    return (activated, grad_weight, grad_features)


def solution(mesh):
    return jax.shard_map(
        per_device,
        mesh=mesh,
        in_specs=(
            P("col", "row", None),
            P(),
            P(("row", "col"), None),
            P("row", "col", None, None, None),
            P("row", "col", None),
            P("row", "col", None),
            P("row", "col"),
        ),
        out_specs=(P(("row", "col"), None), P(), P("col", "row", None)),
        check_vma=False,
    )
```

```python
import functools

import jax
import jax.numpy as jnp
from jax import lax
from jax.experimental import pallas as pl
from jax.experimental.pallas import tpu as pltpu
from jax.sharding import PartitionSpec as P

BF16 = jnp.bfloat16
F32 = jnp.float32
UNROLL = 32
MIB = 1 << 20


def start_lists(sources, targets, sems):
    copies = [
        pltpu.make_async_copy(source, target, sems.at[at])
        for at, (source, target) in enumerate(zip(sources, targets))
    ]
    for copy in copies:
        copy.start()
    return copies


def start_chunks(live, vals_hbm, vals, sems, chunk):
    for piece in range(vals.shape[0] // chunk):

        @pl.when(piece * chunk < live)
        def _():
            part = pl.ds(piece * chunk, chunk)
            pltpu.make_async_copy(vals_hbm.at[part], vals.at[part], sems.at[piece]).start()


def each_live_slot(live, vals_hbm, vals, sems, chunk, one_slot):
    def one_chunk(piece, unused):
        part = pl.ds(piece * chunk, chunk)
        pltpu.make_async_copy(vals_hbm.at[part], vals.at[part], sems.at[piece]).wait()

        def one_group(group, unused):
            for lane in range(UNROLL):
                slot = piece * chunk + group * UNROLL + lane
                one_slot(slot, slot < live)
            return unused

        groups = (jnp.minimum(chunk, live - piece * chunk) + UNROLL - 1) // UNROLL
        return lax.fori_loop(0, groups, one_group, unused)

    lax.fori_loop(0, (live + chunk - 1) // chunk, one_chunk, 0)


def forward_kernel(chunk, steps, place, count, rows_hbm, cols_hbm, vals_hbm, *refs):
    n_row = len(refs) - 10
    pieces = refs[:n_row]
    send, keep, rows, cols, vals, panel, total, index_sems, val_sems, piece_sems = refs[n_row:]
    core, row, live = place[0], place[1], count[0]
    blocks_here = pieces[0].shape[0]
    copies = start_lists((rows_hbm, cols_hbm), (rows, cols), index_sems)
    for at, (step, piece) in enumerate(zip(steps, pieces)):
        owner = lax.rem(row + n_row - step, n_row)
        copies.append(
            pltpu.make_async_copy(
                piece, panel.at[pl.ds(owner * blocks_here, blocks_here)], piece_sems.at[at]
            )
        )
        copies[-1].start()
    start_chunks(live, vals_hbm, vals, val_sems, chunk)
    spare = total.shape[0] - 1

    def clear(block, unused):
        total[block] = jnp.zeros(total.shape[1:], F32)
        return unused

    lax.fori_loop(0, spare, clear, 0)
    for copy in copies:
        copy.wait()

    def one_slot(slot, alive):
        target = jnp.where(alive, rows[slot], spare)
        total[target] += jnp.dot(vals[slot], panel[cols[slot]], preferred_element_type=F32)

    each_live_slot(live, vals_hbm, vals, val_sems, chunk, one_slot)
    side, width = total.shape[1:]

    def split(chip, unused):
        first = 2 * blocks_here * chip
        other = total[pl.ds(first + blocks_here * (1 - core), blocks_here)]
        mine = total[pl.ds(first + blocks_here * core, blocks_here)]
        send[chip] = other.reshape(blocks_here * side, width).astype(BF16)
        keep[chip] = mine.reshape(blocks_here * side, width)
        return unused

    lax.fori_loop(0, send.shape[0], split, 0)


def backward_kernel(chunk, steps, place, count, rows_hbm, cols_hbm, vals_hbm, same, other, *refs):
    n_row = len(steps)
    outs = refs[:n_row]
    rows, cols, vals, grads, total, index_sems, val_sems, grad_sems = refs[n_row:]
    core, row, live = place[0], place[1], count[0]
    side = total.shape[1]
    copies = [
        pltpu.make_async_copy(same, grads.at[core], grad_sems.at[0]),
        pltpu.make_async_copy(other, grads.at[1 - core], grad_sems.at[1]),
    ]
    for copy in copies:
        copy.start()
    copies += start_lists((rows_hbm, cols_hbm), (rows, cols), index_sems)
    start_chunks(live, vals_hbm, vals, val_sems, chunk)
    spare = total.shape[0] - 1
    for block in range(spare):
        total[block] = jnp.zeros(total.shape[1:], F32)
    for copy in copies:
        copy.wait()

    def one_slot(slot, alive):
        target = jnp.where(alive, cols[slot], spare)
        block = rows[slot]
        first = pl.multiple_of((block & 1) * side, side)
        picked = grads[(block >> 1) & 1, block >> 2, pl.ds(first, side)]
        total[target] += lax.dot_general(
            vals[slot], picked, (((0,), (0,)), ((), ())), preferred_element_type=F32
        )

    each_live_slot(live, vals_hbm, vals, val_sems, chunk, one_slot)
    blocks_here = spare // n_row
    for step, out in zip(steps, outs):
        owner = lax.rem(row + step, n_row)
        mine = total[pl.ds(owner * blocks_here, blocks_here)]
        out[...] = mine.reshape(out.shape).astype(BF16)


def dense_kernel(parts, weight, cotangent, activated, grad_agg):
    total = parts[0].astype(F32)
    for chip in range(1, parts.shape[0]):
        total += parts[chip].astype(F32)
    aggregated = total.astype(BF16)
    pre = jnp.dot(aggregated, weight[...], preferred_element_type=F32)
    sigma = jax.nn.sigmoid(pre)
    activated[...] = (pre * sigma).astype(BF16)
    grad_pre = (cotangent[...].astype(F32) * sigma * (1.0 + pre * (1.0 - sigma))).astype(BF16)
    local_weight = lax.dot_general(
        aggregated, grad_pre, (((0,), (0,)), ((), ())), preferred_element_type=F32
    ).astype(BF16)
    grad = lax.dot_general(
        grad_pre, weight[...], (((1,), (1,)), ((), ())), preferred_element_type=F32
    ).astype(BF16)
    nodes = grad.shape[0]
    strip = grad_agg.shape[1] - nodes
    for chip in range(grad_agg.shape[0]):
        grad_agg[chip, :nodes] = grad
        grad_agg[chip, nodes:] = local_weight[chip * strip : (chip + 1) * strip]


def turn(size, step):
    return [(i, (i + step) % size) for i in range(size)]


def per_device(features, weight, cotangent, blk_vals, blk_rows, blk_cols, blk_count):
    n_row, n_col = lax.axis_size("row"), lax.axis_size("col")
    nodes, width = cotangent.shape
    slots, side = blk_vals.shape[2], blk_vals.shape[3]
    here = nodes // side
    chips = n_col // 2
    chunk = slots // 6
    place = jnp.stack([lax.axis_index("col") % 2, lax.axis_index("row")]).astype(jnp.int32)
    in_hbm = functools.partial(pltpu.with_memory_space_constraint, memory_space=pltpu.HBM)
    scalars = (place, blk_count[0], in_hbm(blk_rows[0, 0]), in_hbm(blk_cols[0, 0]))
    values = in_hbm(blk_vals[0, 0])
    smem = pl.BlockSpec(memory_space=pltpu.SMEM)
    vmem = pl.BlockSpec(memory_space=pltpu.VMEM)
    near = pl.BlockSpec(memory_space=pl.ANY)
    hbm = pl.BlockSpec(memory_space=pltpu.HBM)
    swap = [(i, i ^ 1) for i in range(n_col)]
    same_core = [list(range(core, n_col, 2)) for core in range(2)]
    work = 2 * slots * side * side * width

    own = features.reshape(here, side, width)
    steps = [0] + sorted(range(1, n_row), key=lambda k: (min(k, n_row - k), k))
    arrival = [0] + steps[:0:-1]
    pieces = [in_hbm(own)] + [lax.ppermute(own, "row", turn(n_row, k)) for k in arrival[1:]]

    send, keep = pl.pallas_call(
        functools.partial(forward_kernel, chunk, arrival),
        out_shape=(
            jax.ShapeDtypeStruct((chips, nodes, width), BF16),
            jax.ShapeDtypeStruct((chips, nodes, width), F32),
        ),
        in_specs=[smem] * 2 + [hbm] * 4 + [near] * (n_row - 1),
        out_specs=(vmem, vmem),
        scratch_shapes=[
            pltpu.SMEM((slots,), jnp.int32),
            pltpu.SMEM((slots,), jnp.int32),
            pltpu.VMEM((slots, side, side), BF16),
            pltpu.VMEM((here * n_row, side, width), BF16),
            pltpu.VMEM((here * n_col + 1, side, width), F32),
            pltpu.SemaphoreType.DMA((2,)),
            pltpu.SemaphoreType.DMA((slots // chunk,)),
            pltpu.SemaphoreType.DMA((n_row,)),
        ],
        compiler_params=pltpu.CompilerParams(vmem_limit_bytes=40 * MIB),
        cost_estimate=pl.CostEstimate(flops=work, bytes_accessed=14 * MIB, transcendentals=0),
    )(*scalars, values, *pieces)

    arrived = lax.ppermute(send, "col", swap)
    shares = (keep + arrived.astype(F32)).astype(BF16)
    parts = lax.all_to_all(shares, "col", 0, 0, tiled=True, axis_index_groups=same_core)

    strip = width // chips
    activated, grad_agg = pl.pallas_call(
        dense_kernel,
        out_shape=(
            jax.ShapeDtypeStruct((nodes, width), BF16),
            jax.ShapeDtypeStruct((chips, nodes + strip, width), BF16),
        ),
        in_specs=[vmem] * 3,
        out_specs=(vmem,) * 2,
        compiler_params=pltpu.CompilerParams(vmem_limit_bytes=24 * MIB),
        cost_estimate=pl.CostEstimate(
            flops=6 * nodes * width * width, bytes_accessed=5 * MIB, transcendentals=nodes * width
        ),
    )(parts, weight, cotangent)

    same = lax.all_to_all(grad_agg, "col", 0, 0, tiled=True, axis_index_groups=same_core)
    other = lax.ppermute(same, "col", swap)
    strips = jnp.sum(same[:, nodes:].astype(F32), axis=0)
    copies = jnp.broadcast_to(strips[None], (n_row, strip, width))
    strips = lax.all_to_all(copies, "row", 0, 0, tiled=True)

    shares = pl.pallas_call(
        functools.partial(backward_kernel, chunk, steps),
        out_shape=(jax.ShapeDtypeStruct((nodes, width), BF16),) * n_row,
        in_specs=[smem] * 2 + [hbm] * 3 + [near] * 2,
        out_specs=(vmem,) * n_row,
        scratch_shapes=[
            pltpu.SMEM((slots,), jnp.int32),
            pltpu.SMEM((slots,), jnp.int32),
            pltpu.VMEM((slots, side, side), BF16),
            pltpu.VMEM((2, chips, nodes + strip, width), BF16),
            pltpu.VMEM((here * n_row + 1, side, width), F32),
            pltpu.SemaphoreType.DMA((2,)),
            pltpu.SemaphoreType.DMA((slots // chunk,)),
            pltpu.SemaphoreType.DMA((2,)),
        ],
        compiler_params=pltpu.CompilerParams(vmem_limit_bytes=40 * MIB),
        cost_estimate=pl.CostEstimate(flops=work, bytes_accessed=11 * MIB, transcendentals=0),
    )(*scalars, values, same, other)

    shares, strips = lax.optimization_barrier((shares, strips))
    order = list(zip(steps, shares))[::-1]
    far, close, own_share = order[: n_row // 2], order[n_row // 2 : -1], shares[0]
    moved = [lax.ppermute(share, "row", turn(n_row, step)) for step, share in far]
    copies = jnp.broadcast_to(jnp.sum(strips, axis=0)[None], (n_col, strip, width))
    every = lax.all_to_all(copies, "col", 0, 0, tiled=True)
    every, held = lax.optimization_barrier((every, [share for unused, share in close]))
    moved += [
        lax.ppermute(share, "row", turn(n_row, step)) for (step, unused), share in zip(close, held)
    ]
    total = own_share.astype(F32)
    for share in moved:
        total += share.astype(F32)
    grad_features = total.astype(BF16).reshape(1, nodes, width)
    grad_weight = jnp.sum(every.reshape(chips, 2, strip, width), axis=1).reshape(width, width)
    return (activated, grad_weight, grad_features)


def solution(mesh):
    return jax.shard_map(
        per_device,
        mesh=mesh,
        in_specs=(
            P("col", "row", None),
            P(),
            P(("row", "col"), None),
            P("row", "col", None, None, None),
            P("row", "col", None),
            P("row", "col", None),
            P("row", "col"),
        ),
        out_specs=(P(("row", "col"), None), P(), P("col", "row", None)),
        check_vma=False,
    )
```
